32 devices in a mesh: row: 4 (over z), col: 8 (over y, x, core).
Axes of the slice: x: 2, y: 2, z: 4, core: 2. Of those that a mesh axis runs over, the one named last changes fastest.
Arguments:
- trailing: float32 [16384, 16384], P('row', 'col'), may hold values from -6 to 6
- panel_factors: float32 [1024, 16384], P('col', 'row'), may hold values from -1.2 to 1.2
- vectors_t: float32 [16, 64, 512], P('col'), may hold values from -0.25 to 0.25
- inverse_lower_factors: float32 [16, 512, 512], P('col', 'row'), as said below
- slot_of_panel: int32 [16], replicated, may hold values from 0 to 15, each once
Outputs:
- updated: float32 [16384, 16384], P('row', 'col')
The draws below stay inside these ranges and needn't reach their ends.
Inputs may be any that keep to these rules, and one draw needn't show every extreme that they name: `slot_of_panel`: a permutation of the panels' slots. `inverse_lower_factors`: each slot's matrix is lower triangular with a positive diagonal.
All inputs are finite; a program needn't handle non-finite values.
Results may differ from the reference program's by a relative error of at most 0.000075.
Values sent between devices are 32-bit elements; how exact they have to be, the bound alone decides.
No kernel may reach another device: no remote copies, remote signals or barrier semaphores. Data moves between devices by JAX's collectives and lax.ppermute only.
A program may use at most 256 MiB of HBM per device.

```python
import math
import jax
import jax.numpy as jnp
from jax import lax

ORDER = 16384
TILE = 512
RANK = 64
PANELS = 16


def draw_inverse_lower_factors(key, part):
    first, second, third = jax.random.split(jax.random.fold_in(key, 7), 3)
    rough = jax.random.normal(first, (PANELS, TILE, TILE), jnp.float32) * (0.6 / math.sqrt(TILE))
    diagonal_tile = jax.random.uniform(second, (PANELS, TILE), jnp.float32, 0.5, 2.0)
    factor = jnp.exp(jax.random.uniform(third, (PANELS, 1, 1), jnp.float32, -0.7, 0.7))
    lower = jnp.tril(rough, -1) + diagonal_tile[:, :, None] * jnp.eye(TILE, dtype=jnp.float32)[None, :, :]
    return lower * factor


def level_of(key, dims, pieces, low, high):
    def one(axis_at, shards_of):
        draws = jax.random.uniform(jax.random.fold_in(jax.random.fold_in(key, 6), axis_at), (shards_of,), jnp.float32, low / len(pieces), high / len(pieces))
        return jnp.repeat(jnp.exp(draws), dims[axis_at] // shards_of).reshape((-1,) + (1,) * (len(dims) - axis_at - 1))

    loudness = one(*pieces[0])
    for cut in pieces[1:]:
        loudness = loudness * one(*cut)
    return loudness


def scatter_about(key, shape, spread, most, cuts=(), kind=jnp.bfloat16):
    values = jax.random.normal(key, shape, jnp.float32) * spread
    if len(cuts) > 0:
        values = level_of(key, shape, cuts, -0.22, 0.18) * values
    return jnp.clip(values, min=-most, max=most).astype(kind)


def setup_inputs(seed: int = 0) -> dict:
    key_of = jax.random.split(jax.random.key(seed), 6)
    trailing = scatter_about(key_of[0], (ORDER, ORDER), 1.0, 6.0, ((0, 4), (1, 8)), jnp.float32)
    panel_factors = scatter_about(key_of[1], (PANELS * RANK, ORDER), 0.18, 1.2, ((0, 8), (1, 4)), jnp.float32)
    vectors_t = scatter_about(key_of[2], (PANELS, RANK, TILE), TILE ** -0.5, 0.25, ((0, 8),), jnp.float32)
    inverse_lower_factors = draw_inverse_lower_factors(jax.random.fold_in(key_of[5], 71), 0)
    slot_of_panel = jax.random.permutation(key_of[4], PANELS).astype(jnp.int32)
    return {"trailing": trailing, "panel_factors": panel_factors, "vectors_t": vectors_t, "inverse_lower_factors": inverse_lower_factors, "slot_of_panel": slot_of_panel}


def reference(trailing, panel_factors, vectors_t, inverse_lower_factors, slot_of_panel):
    highest_precision = lax.Precision.HIGHEST
    solved_panel = jnp.einsum("sat,srt->sar", vectors_t, inverse_lower_factors, precision=highest_precision)
    core_blocks = jnp.einsum("fdv,fpv->fdp", solved_panel, solved_panel, precision=highest_precision)
    panel_cores = core_blocks[slot_of_panel.astype(jnp.int32)]
    reshaped_block = panel_factors.reshape(PANELS, RANK, ORDER)
    scaled = jnp.einsum("pab,pbi->pai", panel_cores, reshaped_block, precision=highest_precision).reshape(PANELS * RANK, ORDER)
    update = lax.dot_general(scaled, panel_factors, (((0,), (0,)), ((), ())), precision=highest_precision)
    return trailing - update
```

```python
import functools

import jax
import jax.numpy as jnp
from jax import lax
from jax.experimental import pallas as pl
from jax.experimental.pallas import tpu as pltpu
from jax.sharding import PartitionSpec as P

CHUNKS = 4
HIGHEST = lax.Precision.HIGHEST
VMEM_LIMIT = 48 * 1024 * 1024


def split(x):
    hi = x.astype(jnp.bfloat16)
    return hi, (x - hi.astype(jnp.float32)).astype(jnp.bfloat16)


def scale_kernel(place, first, second, cores, *refs):
    hi, lo = refs[-2:]
    pair = jnp.concatenate([first[...], second[...]], axis=0)
    scaled = jnp.dot(cores[...], pair, precision=HIGHEST, preferred_element_type=jnp.float32)
    hi[...], lo[...] = split(scaled.T)


def scale_into(place, first, second, cores, previous, depth):
    rows, width = first.shape
    tile = min(width, 1024)
    block = pl.BlockSpec((tile, 2 * rows), lambda i, place: (i, place[0]))
    shape = jax.ShapeDtypeStruct((width, depth), jnp.bfloat16)
    part = pl.BlockSpec((rows, tile), lambda i, place: (0, i))
    held = [] if previous is None else list(previous)
    return pl.pallas_call(
        scale_kernel,
        grid_spec=pltpu.PrefetchScalarGridSpec(
            num_scalar_prefetch=1,
            grid=(width // tile,),
            in_specs=[part, part, pl.BlockSpec((2 * rows, 2 * rows), lambda i, place: (0, 0))]
            + [pl.BlockSpec(memory_space=pl.ANY)] * len(held),
            out_specs=[block, block],
        ),
        out_shape=[shape, shape],
        input_output_aliases={} if previous is None else {4: 0, 5: 1},
        compiler_params=pltpu.CompilerParams(vmem_limit_bytes=VMEM_LIMIT),
        cost_estimate=pl.CostEstimate(
            flops=6 * 2 * width * 4 * rows * rows, bytes_accessed=16 * rows * width, transcendentals=0
        ),
    )(place, first, second, cores, *held)


def update_kernel(count, trailing, hi, lo, *refs):
    parts, (out, right_hi, right_lo) = refs[:count], refs[-3:]

    @pl.when(pl.program_id(0) == 0)
    def _():
        at = 0
        for part in parts:
            rows = part.shape[0]
            right_hi[at : at + rows, :], right_lo[at : at + rows, :] = split(part[...])
            at += rows

    dot = functools.partial(jnp.dot, preferred_element_type=jnp.float32)
    total = dot(hi[...], right_hi[...]) + (dot(hi[...], right_lo[...]) + dot(lo[...], right_hi[...]))
    out[...] = trailing[...] - total


def update_chunk(chunk, trailing, left, parts, previous):
    height, width = trailing.shape
    depth = left[0].shape[1]
    wide = width // CHUNKS
    tile = min(height, 512)
    here = pl.BlockSpec((tile, wide), lambda i: (i, chunk))
    side = pl.BlockSpec((tile, depth), lambda i: (i, 0))
    specs = [
        pl.BlockSpec((a.shape[0], wide), (lambda i: (0, 0)) if alone else (lambda i: (0, chunk)))
        for a, alone in parts
    ]
    held = [] if previous is None else [previous]
    return pl.pallas_call(
        functools.partial(update_kernel, len(parts)),
        grid=(height // tile,),
        in_specs=[here, side, side] + specs + [pl.BlockSpec(memory_space=pl.ANY)] * len(held),
        out_specs=here,
        out_shape=jax.ShapeDtypeStruct(trailing.shape, jnp.float32),
        scratch_shapes=[pltpu.VMEM((depth, wide), jnp.bfloat16)] * 2,
        input_output_aliases={} if previous is None else {3 + len(parts): 0},
        compiler_params=pltpu.CompilerParams(vmem_limit_bytes=VMEM_LIMIT),
        cost_estimate=pl.CostEstimate(
            flops=3 * 2 * height * wide * depth,
            bytes_accessed=8 * height * wide + 4 * height * depth + 4 * wide * depth,
            transcendentals=0,
        ),
    )(trailing, *left, *(a for a, _ in parts), *held)


def body(planes, columns, trailing, panel_factors, vectors_t, inverse_lower_factors, slot_of_panel):
    lines = columns // 2
    per_col, rank, _ = vectors_t.shape
    panels = per_col * columns
    rows = panel_factors.shape[0]
    width = trailing.shape[1]
    wide = width // CHUNKS
    depth = rows * columns
    z = lax.axis_index("row")
    col = lax.axis_index("col")
    line, core = col // 2, col % 2

    def device(plane, on_line, on_core):
        return plane * columns + 2 * on_line + on_core

    def permute(x, pairs):
        moves = [
            (device(*source, k), device(*target, k ^ flip)) for source, target, flip in pairs for k in range(2)
        ]
        return lax.ppermute(x, ("row", "col"), moves)

    def across(x, bits):
        return lax.ppermute(x, "col", [(i, i ^ bits) for i in range(columns)])

    def half(x, which):
        return lax.dynamic_slice_in_dim(x, which * width, width, axis=1)

    same = half(panel_factors, core)
    other = half(panel_factors, 1 - core)
    swapped = across(other, 1)

    down = [((q, q), (q - 1, q), 0) for q in range(1, planes)]
    up = [((q, q), (q + 1, q), 0) for q in range(planes - 1)]

    def onward(d):
        lower = [((q - d + 1, q), (q - d, q), 0) for q in range(d, planes)]
        return lower + [((q + d - 1, q), (q + d, q), 0) for q in range(planes - d)]

    def along(to_lower, to_upper, mine):
        got = permute(to_lower, down) + permute(to_upper, up)
        total = got
        for d in range(2, planes):
            got = permute(got, onward(d))
            total = total + got
        return jnp.where(z == line, mine, total)

    gathered = [[panel_factors, None]] + [[None, None] for _ in range(lines - 1)]
    for s in sorted(range(1, lines), key=lambda s: bin(s).count("1")):
        low, high = s & -s, 1 << (s.bit_length() - 1)
        if low == high:
            gathered[s][0] = across(panel_factors, 2 * s)
        else:
            cut = rows // 2
            gathered[s][0] = jnp.concatenate(
                [
                    across(gathered[s ^ high][0][:cut], 2 * high),
                    across(gathered[s ^ low][0][cut:], 2 * low),
                ]
            )
    for s in range(lines):
        gathered[s][1] = across(gathered[s][0], 1)

    first_skip, last_skip = line, line ^ (lines - 1)
    low_kind = jnp.logical_or(z < line, jnp.logical_and(z == line, line != 0))
    skip = jnp.where(low_kind, first_skip, last_skip)
    crossed = [None, None]
    a_same, a_other = same, other
    for d in range(1, planes):
        pairs = [((p, 0), (p - 1, 0), 0) for p in range(1, planes - d + 1)]
        pairs += [((p, lines - 1), (p + 1, lines - 1), 0) for p in range(d - 1, planes - 1)]
        a_same, a_other = permute(a_same, pairs), permute(a_other, pairs)
        for k, a in enumerate((a_same, a_other)):
            hop = [((p, 0), (p, p + d), k) for p in range(planes - d)]
            hop += [((p, lines - 1), (p, p - d), k) for p in range(d, planes)]
            got = permute(a, hop)
            crossed[k] = got if crossed[k] is None else crossed[k] + got
    kept = []
    for k in range(2):
        mine = half(gathered[1][k], core)
        for s in range(2, lines):
            mine = jnp.where(skip == s, half(gathered[s][k], core), mine)
        kept.append(jnp.where(z == line, mine, crossed[k]))

    own = [along(same, same, same), along(swapped, swapped, swapped)]

    def others(skipped, chunk):
        at = core * width + chunk * wide
        blocks = []
        for i in range(lines - 2):
            for k in range(2):
                near, far = (
                    lax.dynamic_slice_in_dim(gathered[s][k], at, wide, axis=1) for s in (i + 1, i + 2)
                )
                blocks.append(jnp.where(i + 1 < skipped, near, far))
        return jnp.concatenate(blocks)

    rest = []
    for chunk in range(CHUNKS):
        to_lower, to_upper = others(first_skip, chunk), others(last_skip, chunk)
        rest.append(along(to_lower, to_upper, jnp.where(line != 0, to_lower, to_upper)))

    solved = lax.dot_general(
        vectors_t, inverse_lower_factors, (((2,), (2,)), ((0,), (0,))), precision=HIGHEST
    )
    cores = jnp.einsum("fdv,fpv->fdp", solved, solved, precision=HIGHEST)
    bit = 1
    while bit < planes:
        cores = cores + lax.ppermute(cores, "row", [(i, i ^ bit) for i in range(planes)])
        bit *= 2
    bit = 1
    while bit < columns:
        cores = jnp.concatenate([cores, across(cores, bit)])
        bit *= 2
    owner = col ^ jnp.arange(columns, dtype=jnp.int32)
    panel = (owner[:, None] * per_col + jnp.arange(per_col, dtype=jnp.int32)[None, :]).reshape(panels)
    slot = slot_of_panel[panel]
    panel_cores = cores[(slot // per_col ^ col) * per_col + slot % per_col]
    together = 2 * per_col
    diagonal = jnp.eye(together, dtype=jnp.float32)
    blocks = (
        panel_cores.reshape(lines, together, rank, 1, rank) * diagonal[None, :, None, :, None]
    ).reshape(lines, together * rank, together * rank)

    left = None
    for s in range(lines):
        if s == 0:
            place = jnp.int32(0)
        else:
            place = jnp.where(s == skip, lines - 1, jnp.where(s < skip, s, s - 1))
        left = scale_into(
            place.astype(jnp.int32).reshape(1), gathered[s][0], gathered[s][1], blocks[s], left, depth
        )

    updated = None
    for chunk in range(CHUNKS):
        parts = [(own[0], False), (own[1], False), (rest[chunk], True), (kept[0], False), (kept[1], False)]
        updated = update_chunk(chunk, trailing, left, parts, updated)
    return updated


def solution(mesh):
    planes, columns = mesh.shape["row"], mesh.shape["col"]
    if columns != 2 * planes or planes & (planes - 1):
        raise ValueError("unsupported mesh")
    return jax.shard_map(
        functools.partial(body, planes, columns),
        mesh=mesh,
        in_specs=(
            P("row", "col"),
            P("col", "row"),
            P("col", None, None),
            P("col", "row", None),
            P(),
        ),
        out_specs=P("row", "col"),
        check_vma=False,
    )
```

```python
import functools

import jax
import jax.numpy as jnp
from jax import lax
from jax.experimental import pallas as pl
from jax.experimental.pallas import tpu as pltpu
from jax.sharding import PartitionSpec as P

EIGHTHS = (2, 2, 2, 1, 1)
HIGHEST = lax.Precision.HIGHEST
VMEM_LIMIT = 48 * 1024 * 1024


def split(x):
    hi = x.astype(jnp.bfloat16)
    return hi, (x - hi.astype(jnp.float32)).astype(jnp.bfloat16)


def scale_kernel(place, first, second, cores, *refs):
    hi, lo = refs[-2:]
    pair = jnp.concatenate([first[...], second[...]], axis=0)
    scaled = jnp.dot(cores[...], pair, precision=HIGHEST, preferred_element_type=jnp.float32)
    hi[...], lo[...] = split(scaled.T)


def scale_into(place, first, second, cores, previous, depth):
    rows, width = first.shape
    tile = min(width, 1024)
    block = pl.BlockSpec((tile, 2 * rows), lambda i, place: (i, place[0]))
    shape = jax.ShapeDtypeStruct((width, depth), jnp.bfloat16)
    part = pl.BlockSpec((rows, tile), lambda i, place: (0, i))
    held = [] if previous is None else list(previous)
    return pl.pallas_call(
        scale_kernel,
        grid_spec=pltpu.PrefetchScalarGridSpec(
            num_scalar_prefetch=1,
            grid=(width // tile,),
            in_specs=[part, part, pl.BlockSpec((2 * rows, 2 * rows), lambda i, place: (0, 0))]
            + [pl.BlockSpec(memory_space=pl.ANY)] * len(held),
            out_specs=[block, block],
        ),
        out_shape=[shape, shape],
        input_output_aliases={} if previous is None else {4: 0, 5: 1},
        compiler_params=pltpu.CompilerParams(vmem_limit_bytes=VMEM_LIMIT),
        cost_estimate=pl.CostEstimate(
            flops=6 * 2 * width * 4 * rows * rows, bytes_accessed=16 * rows * width, transcendentals=0
        ),
    )(place, first, second, cores, *held)


def update_kernel(trailing, hi, lo, right, *refs):
    out, right_hi, right_lo = refs[-3:]

    @pl.when(pl.program_id(0) == 0)
    def _():
        right_hi[...], right_lo[...] = split(right[...])

    dot = functools.partial(jnp.dot, preferred_element_type=jnp.float32)
    total = dot(hi[...], right_hi[...]) + (dot(hi[...], right_lo[...]) + dot(lo[...], right_hi[...]))
    out[...] = trailing[...] - total


def update_chunk(start, trailing, left, right, previous):
    height = trailing.shape[0]
    depth, wide = right.shape
    tile = min(height, 1024)
    here = pl.BlockSpec((tile, wide), lambda i: (i, start // wide))
    side = pl.BlockSpec((tile, depth), lambda i: (i, 0))
    held = [] if previous is None else [previous]
    return pl.pallas_call(
        update_kernel,
        grid=(height // tile,),
        in_specs=[here, side, side, pl.BlockSpec((depth, wide), lambda i: (0, 0))]
        + [pl.BlockSpec(memory_space=pl.ANY)] * len(held),
        out_specs=here,
        out_shape=jax.ShapeDtypeStruct(trailing.shape, jnp.float32),
        scratch_shapes=[pltpu.VMEM((depth, wide), jnp.bfloat16)] * 2,
        input_output_aliases={} if previous is None else {4: 0},
        compiler_params=pltpu.CompilerParams(vmem_limit_bytes=VMEM_LIMIT),
        cost_estimate=pl.CostEstimate(
            flops=3 * 2 * height * wide * depth,
            bytes_accessed=8 * height * wide + 4 * height * depth + 4 * wide * depth,
            transcendentals=0,
        ),
    )(trailing, *left, right, *held)


def body(planes, columns, trailing, panel_factors, vectors_t, inverse_lower_factors, slot_of_panel):
    lines = columns // 2
    per_col, rank, _ = vectors_t.shape
    panels = per_col * columns
    rows = panel_factors.shape[0]
    width = trailing.shape[1]
    depth = rows * columns
    halves = columns // planes
    col = lax.axis_index("col")
    line, core = col // 2, col % 2

    def across(x, bits):
        return lax.ppermute(x, "col", [(i, i ^ bits) for i in range(columns)])

    solved = lax.dot_general(
        vectors_t, inverse_lower_factors, (((2,), (2,)), ((0,), (0,))), precision=HIGHEST
    )
    cores = jnp.einsum("fdv,fpv->fdp", solved, solved, precision=HIGHEST)
    bit = 1
    while bit < planes:
        cores = cores + lax.ppermute(cores, "row", [(i, i ^ bit) for i in range(planes)])
        bit *= 2
    bit = 1
    while bit < columns:
        cores = jnp.concatenate([cores, across(cores, bit)])
        bit *= 2
    bulk, cores = lax.optimization_barrier((panel_factors, cores))

    split_columns = panel_factors.reshape(rows, halves, width)
    starts, chunks = [], []
    at = 0
    for eighths in EIGHTHS:
        wide = eighths * width // 8
        mine = jnp.stack([split_columns[:, h, at : at + wide] for h in range(halves)])
        everywhere = lax.all_gather(mine, "row", axis=0, tiled=True)
        chunk = lax.all_to_all(everywhere, "col", split_axis=0, concat_axis=0, tiled=True)
        starts.append(at)
        chunks.append(chunk.reshape(depth, wide))
        at += wide

    gathered = [[bulk, None]] + [[None, None] for _ in range(lines - 1)]
    for s in sorted(range(1, lines), key=lambda s: bin(s).count("1")):
        low, high = s & -s, 1 << (s.bit_length() - 1)
        if low == high:
            gathered[s][0] = across(bulk, 2 * s)
        else:
            cut = rows // 2
            gathered[s][0] = jnp.concatenate(
                [
                    across(gathered[s ^ high][0][:cut], 2 * high),
                    across(gathered[s ^ low][0][cut:], 2 * low),
                ]
            )
    for s in range(lines):
        gathered[s][1] = across(gathered[s][0], 1)

    owner = col ^ jnp.arange(columns, dtype=jnp.int32)
    panel = (owner[:, None] * per_col + jnp.arange(per_col, dtype=jnp.int32)[None, :]).reshape(panels)
    slot = slot_of_panel[panel]
    panel_cores = cores[(slot // per_col ^ col) * per_col + slot % per_col]
    together = 2 * per_col
    diagonal = jnp.eye(together, dtype=jnp.float32)
    blocks = (
        panel_cores.reshape(lines, together, rank, 1, rank) * diagonal[None, :, None, :, None]
    ).reshape(lines, together * rank, together * rank)
    blocks = jnp.where(core == 0, blocks, jnp.roll(blocks, rows, axis=1))

    left = None
    for s in range(lines):
        place = (line ^ s).astype(jnp.int32).reshape(1)
        left = scale_into(place, gathered[s][0], gathered[s][1], blocks[s], left, depth)

    updated = None
    for start, chunk in zip(starts, chunks):
        updated = update_chunk(start, trailing, left, chunk, updated)
    return updated


def solution(mesh):
    planes, columns = mesh.shape["row"], mesh.shape["col"]
    if columns != 2 * planes or planes & (planes - 1):
        raise ValueError("unsupported mesh")
    return jax.shard_map(
        functools.partial(body, planes, columns),
        mesh=mesh,
        in_specs=(
            P("row", "col"),
            P("col", "row"),
            P("col", None, None),
            P("col", "row", None),
            P(),
        ),
        out_specs=P("row", "col"),
        check_vma=False,
    )
```

```python
import functools

import jax
import jax.numpy as jnp
from jax import lax
from jax.experimental import pallas as pl
from jax.experimental.pallas import tpu as pltpu
from jax.sharding import PartitionSpec as P

CHUNKS = ((0, 3), (4, 2), (6, 2), (3, 1))
HIGHEST = lax.Precision.HIGHEST
SCALE_VMEM = 16 * 1024 * 1024
UPDATE_VMEM = 20 * 1024 * 1024


def split(x):
    hi = x.astype(jnp.bfloat16)
    return hi, (x - hi.astype(jnp.float32)).astype(jnp.bfloat16)


def scale_kernel(place, first, second, cores, *refs):
    hi, lo = refs[-2:]
    pair = jnp.concatenate([first[...], second[...]], axis=0)
    scaled = jnp.dot(cores[...], pair, precision=HIGHEST, preferred_element_type=jnp.float32)
    hi[...], lo[...] = split(scaled.T)


def scale_into(place, first, second, cores, previous, depth):
    rows, width = first.shape
    tile = min(width, 1024)
    block = pl.BlockSpec((tile, 2 * rows), lambda i, place: (i, place[0]))
    shape = jax.ShapeDtypeStruct((width, depth), jnp.bfloat16)
    part = pl.BlockSpec((rows, tile), lambda i, place: (0, i))
    held = [] if previous is None else list(previous)
    return pl.pallas_call(
        scale_kernel,
        grid_spec=pltpu.PrefetchScalarGridSpec(
            num_scalar_prefetch=1,
            grid=(width // tile,),
            in_specs=[part, part, pl.BlockSpec((2 * rows, 2 * rows), lambda i, place: (0, 0))]
            + [pl.BlockSpec(memory_space=pl.ANY)] * len(held),
            out_specs=[block, block],
        ),
        out_shape=[shape, shape],
        input_output_aliases={} if previous is None else {4: 0, 5: 1},
        compiler_params=pltpu.CompilerParams(vmem_limit_bytes=SCALE_VMEM),
        cost_estimate=pl.CostEstimate(
            flops=6 * 2 * width * 4 * rows * rows, bytes_accessed=16 * rows * width, transcendentals=0
        ),
    )(place, first, second, cores, *held)


def update_kernel(trailing, hi, lo, right, *refs):
    out, right_hi, right_lo = refs[-3:]

    @pl.when(pl.program_id(0) == 0)
    def _():
        right_hi[...], right_lo[...] = split(right[...])

    dot = functools.partial(jnp.dot, preferred_element_type=jnp.float32)
    total = dot(hi[...], right_hi[...]) + (dot(hi[...], right_lo[...]) + dot(lo[...], right_hi[...]))
    out[...] = trailing[...] - total


def update_chunk(start, trailing, left, right, previous):
    height = trailing.shape[0]
    depth, wide = right.shape
    tile = min(height, 512)
    here = pl.BlockSpec((tile, wide), lambda i: (i, start // wide))
    side = pl.BlockSpec((tile, depth), lambda i: (i, 0))
    held = [] if previous is None else [previous]
    return pl.pallas_call(
        update_kernel,
        grid=(height // tile,),
        in_specs=[here, side, side, pl.BlockSpec((depth, wide), lambda i: (0, 0))]
        + [pl.BlockSpec(memory_space=pl.ANY)] * len(held),
        out_specs=here,
        out_shape=jax.ShapeDtypeStruct(trailing.shape, jnp.float32),
        scratch_shapes=[pltpu.VMEM((depth, wide), jnp.bfloat16)] * 2,
        input_output_aliases={} if previous is None else {4: 0},
        compiler_params=pltpu.CompilerParams(vmem_limit_bytes=UPDATE_VMEM),
        cost_estimate=pl.CostEstimate(
            flops=3 * 2 * height * wide * depth,
            bytes_accessed=8 * height * wide + 4 * height * depth + 4 * wide * depth,
            transcendentals=0,
        ),
    )(trailing, *left, right, *held)


def body(planes, columns, trailing, panel_factors, vectors_t, inverse_lower_factors, slot_of_panel):
    lines = columns // 2
    per_col, rank, _ = vectors_t.shape
    panels = per_col * columns
    rows = panel_factors.shape[0]
    width = trailing.shape[1]
    depth = rows * columns
    halves = columns // planes
    col = lax.axis_index("col")
    line, core = col // 2, col % 2

    def across(x, bits):
        return lax.ppermute(x, "col", [(i, i ^ bits) for i in range(columns)])

    solved = lax.dot_general(
        vectors_t, inverse_lower_factors, (((2,), (2,)), ((0,), (0,))), precision=HIGHEST
    )
    cores = jnp.einsum("fdv,fpv->fdp", solved, solved, precision=HIGHEST)
    bit = 1
    while bit < columns:
        cores = jnp.concatenate([cores, across(cores, bit)])
        bit *= 2
    bulk, cores = lax.optimization_barrier((panel_factors, cores))
    bit = 1
    while bit < planes:
        cores = cores + lax.ppermute(cores, "row", [(i, i ^ bit) for i in range(planes)])
        bit *= 2

    split_columns = panel_factors.reshape(rows, halves, width)
    starts, chunks = [], []
    for first, eighths in CHUNKS:
        at, wide = first * width // 8, eighths * width // 8
        mine = jnp.stack([split_columns[:, h, at : at + wide] for h in range(halves)])
        everywhere = lax.all_gather(mine, "row", axis=0, tiled=True)
        chunk = lax.all_to_all(everywhere, "col", split_axis=0, concat_axis=0, tiled=True)
        starts.append(at)
        chunks.append(chunk.reshape(depth, wide))

    gathered = [[bulk, None]] + [[None, None] for _ in range(lines - 1)]
    for s in sorted(range(1, lines), key=lambda s: bin(s).count("1")):
        low, high = s & -s, 1 << (s.bit_length() - 1)
        if low == high:
            gathered[s][0] = across(bulk, 2 * s)
        else:
            cut = rows // 2
            gathered[s][0] = jnp.concatenate(
                [
                    across(gathered[s ^ high][0][:cut], 2 * high),
                    across(gathered[s ^ low][0][cut:], 2 * low),
                ]
            )
    for s in range(lines):
        gathered[s][1] = across(gathered[s][0], 1)

    owner = col ^ jnp.arange(columns, dtype=jnp.int32)
    panel = (owner[:, None] * per_col + jnp.arange(per_col, dtype=jnp.int32)[None, :]).reshape(panels)
    slot = slot_of_panel[panel]
    panel_cores = cores[(slot // per_col ^ col) * per_col + slot % per_col]
    together = 2 * per_col
    diagonal = jnp.eye(together, dtype=jnp.float32)
    blocks = (
        panel_cores.reshape(lines, together, rank, 1, rank) * diagonal[None, :, None, :, None]
    ).reshape(lines, together * rank, together * rank)
    blocks = jnp.where(core == 0, blocks, jnp.roll(blocks, rows, axis=1))

    left = None
    for s in range(lines):
        place = (line ^ s).astype(jnp.int32).reshape(1)
        left = scale_into(place, gathered[s][0], gathered[s][1], blocks[s], left, depth)

    updated = None
    for start, chunk in zip(starts, chunks):
        updated = update_chunk(start, trailing, left, chunk, updated)
    return updated


def solution(mesh):
    planes, columns = mesh.shape["row"], mesh.shape["col"]
    if columns != 2 * planes or planes & (planes - 1):
        raise ValueError("unsupported mesh")
    return jax.shard_map(
        functools.partial(body, planes, columns),
        mesh=mesh,
        in_specs=(
            P("row", "col"),
            P("col", "row"),
            P("col", None, None),
            P("col", "row", None),
            P(),
        ),
        out_specs=P("row", "col"),
        check_vma=False,
    )
```

```python
import functools

import jax
import jax.numpy as jnp
from jax import lax
from jax.experimental import pallas as pl
from jax.experimental.pallas import tpu as pltpu
from jax.sharding import PartitionSpec as P

CHUNKS = ((4, 2), (0, 3), (6, 2), (3, 1))
HIGHEST = lax.Precision.HIGHEST
SCALE_VMEM = 48 * 1024 * 1024
UPDATE_VMEM = 48 * 1024 * 1024


def split(x):
    hi = x.astype(jnp.bfloat16)
    return hi, (x - hi.astype(jnp.float32)).astype(jnp.bfloat16)


def scale_kernel(place, first, second, cores, *refs):
    hi, lo = refs[-2:]
    pair = jnp.concatenate([first[...], second[...]], axis=0)
    scaled = jnp.dot(cores[...], pair, precision=HIGHEST, preferred_element_type=jnp.float32)
    hi[...], lo[...] = split(scaled.T)


def scale_into(place, first, second, cores, previous, depth):
    rows, width = first.shape
    tile = min(width, 1024)
    block = pl.BlockSpec((tile, 2 * rows), lambda i, place: (i, place[0]))
    shape = jax.ShapeDtypeStruct((width, depth), jnp.bfloat16)
    part = pl.BlockSpec((rows, tile), lambda i, place: (0, i))
    held = [] if previous is None else list(previous)
    return pl.pallas_call(
        scale_kernel,
        grid_spec=pltpu.PrefetchScalarGridSpec(
            num_scalar_prefetch=1,
            grid=(width // tile,),
            in_specs=[part, part, pl.BlockSpec((2 * rows, 2 * rows), lambda i, place: (0, 0))]
            + [pl.BlockSpec(memory_space=pl.ANY)] * len(held),
            out_specs=[block, block],
        ),
        out_shape=[shape, shape],
        input_output_aliases={} if previous is None else {4: 0, 5: 1},
        compiler_params=pltpu.CompilerParams(vmem_limit_bytes=SCALE_VMEM),
        cost_estimate=pl.CostEstimate(
            flops=6 * 2 * width * 4 * rows * rows, bytes_accessed=16 * rows * width, transcendentals=0
        ),
    )(place, first, second, cores, *held)


def update_kernel(trailing, hi, lo, right, *refs):
    out, right_hi, right_lo = refs[-3:]

    @pl.when(pl.program_id(0) == 0)
    def _():
        right_hi[...], right_lo[...] = split(right[...])

    dot = functools.partial(jnp.dot, preferred_element_type=jnp.float32)
    total = dot(hi[...], right_hi[...]) + (dot(hi[...], right_lo[...]) + dot(lo[...], right_hi[...]))
    out[...] = trailing[...] - total


def update_chunk(start, trailing, left, right, previous):
    height = trailing.shape[0]
    depth, wide = right.shape
    tile = min(height, 512)
    here = pl.BlockSpec((tile, wide), lambda i: (i, start // wide))
    side = pl.BlockSpec((tile, depth), lambda i: (i, 0))
    held = [] if previous is None else [previous]
    return pl.pallas_call(
        update_kernel,
        grid=(height // tile,),
        in_specs=[here, side, side, pl.BlockSpec((depth, wide), lambda i: (0, 0))]
        + [pl.BlockSpec(memory_space=pl.ANY)] * len(held),
        out_specs=here,
        out_shape=jax.ShapeDtypeStruct(trailing.shape, jnp.float32),
        scratch_shapes=[pltpu.VMEM((depth, wide), jnp.bfloat16)] * 2,
        input_output_aliases={} if previous is None else {4: 0},
        compiler_params=pltpu.CompilerParams(vmem_limit_bytes=UPDATE_VMEM),
        cost_estimate=pl.CostEstimate(
            flops=3 * 2 * height * wide * depth,
            bytes_accessed=8 * height * wide + 4 * height * depth + 4 * wide * depth,
            transcendentals=0,
        ),
    )(trailing, *left, right, *held)


def body(planes, columns, trailing, panel_factors, vectors_t, inverse_lower_factors, slot_of_panel):
    lines = columns // 2
    per_col, rank, _ = vectors_t.shape
    panels = per_col * columns
    rows = panel_factors.shape[0]
    width = trailing.shape[1]
    depth = rows * columns
    halves = columns // planes
    col = lax.axis_index("col")
    line, core = col // 2, col % 2

    def across(x, bits):
        return lax.ppermute(x, "col", [(i, i ^ bits) for i in range(columns)])

    def along(x, moves):
        return lax.ppermute(x, "row", moves)

    solved = lax.dot_general(
        vectors_t, inverse_lower_factors, (((2,), (2,)), ((0,), (0,))), precision=HIGHEST
    )
    cores = jnp.einsum("fdv,fpv->fdp", solved, solved, precision=HIGHEST)
    bit = 1
    while bit < planes:
        cores = cores + along(cores, [(i, i ^ bit) for i in range(planes)])
        bit *= 2
    bulk, cores = lax.optimization_barrier((panel_factors, cores))
    near = [cores] + [across(cores, 2 * s) for s in range(1, lines)]
    far = across(jnp.concatenate(near), 1)
    cores = jnp.concatenate([near[0], far[:per_col]] + [
        part for s in range(1, lines) for part in (near[s], far[s * per_col : (s + 1) * per_col])
    ])

    gathered = [[bulk, None]] + [[None, None] for _ in range(lines - 1)]
    for s in sorted(range(1, lines), key=lambda s: bin(s).count("1")):
        low, high = s & -s, 1 << (s.bit_length() - 1)
        if low == high:
            gathered[s][0] = across(bulk, 2 * s)
        else:
            cut = rows // 2
            gathered[s][0] = jnp.concatenate(
                [
                    across(gathered[s ^ high][0][:cut], 2 * high),
                    across(gathered[s ^ low][0][cut:], 2 * low),
                ]
            )
    for s in range(lines):
        gathered[s][1] = across(gathered[s][0], 1)

    chunks = []
    for number, (first, eighths) in enumerate(CHUNKS):
        at, wide = first * width // 8, eighths * width // 8
        source = panel_factors if number == 1 else bulk
        if number == 3:
            source, _ = lax.optimization_barrier((bulk, first_hop))
        source = source.reshape(rows, halves, width)
        mine = jnp.stack([source[:, h, at : at + wide] for h in range(halves)])
        if number == 0:
            lower, upper, line_up = mine, mine, [mine]
            for d in range(1, planes):
                lower = along(lower, [(p, p - 1) for p in range(1, planes - d + 1)])
                upper = along(upper, [(p, p + 1) for p in range(d - 1, planes - 1)])
                line_up = [upper] + line_up + [lower]
            first_hop = line_up[planes]
            everywhere = lax.dynamic_slice_in_dim(
                jnp.concatenate(line_up), halves * (planes - 1 - lax.axis_index("row")), columns
            )
            everywhere, _ = lax.optimization_barrier(
                (everywhere, [gathered[1 << i][0] for i in range(lines.bit_length() - 1)])
            )
        else:
            everywhere = lax.all_gather(mine, "row", axis=0, tiled=True)
        chunk = lax.all_to_all(everywhere, "col", split_axis=0, concat_axis=0, tiled=True)
        chunks.append((at, chunk.reshape(depth, wide)))

    owner = col ^ jnp.arange(columns, dtype=jnp.int32)
    panel = (owner[:, None] * per_col + jnp.arange(per_col, dtype=jnp.int32)[None, :]).reshape(panels)
    slot = slot_of_panel[panel]
    panel_cores = cores[(slot // per_col ^ col) * per_col + slot % per_col]
    together = 2 * per_col
    diagonal = jnp.eye(together, dtype=jnp.float32)
    blocks = (
        panel_cores.reshape(lines, together, rank, 1, rank) * diagonal[None, :, None, :, None]
    ).reshape(lines, together * rank, together * rank)
    blocks = jnp.where(core == 0, blocks, jnp.roll(blocks, rows, axis=1))

    left = None
    for s in range(lines):
        place = (line ^ s).astype(jnp.int32).reshape(1)
        left = scale_into(place, gathered[s][0], gathered[s][1], blocks[s], left, depth)

    updated = None
    for start, chunk in chunks:
        updated = update_chunk(start, trailing, left, chunk, updated)
    return updated


def solution(mesh):
    planes, columns = mesh.shape["row"], mesh.shape["col"]
    if columns != 2 * planes or planes & (planes - 1):
        raise ValueError("unsupported mesh")
    return jax.shard_map(
        functools.partial(body, planes, columns),
        mesh=mesh,
        in_specs=(
            P("row", "col"),
            P("col", "row"),
            P("col", None, None),
            P("col", "row", None),
            P(),
        ),
        out_specs=P("row", "col"),
        check_vma=False,
    )
```

```python
import functools

import jax
import jax.numpy as jnp
from jax import lax
from jax.experimental import pallas as pl
from jax.experimental.pallas import tpu as pltpu
from jax.sharding import PartitionSpec as P

CHUNKS = ((0, 2), (2, 2), (4, 2), (6, 2))
HIGHEST = lax.Precision.HIGHEST
SCALE_VMEM = 48 * 1024 * 1024
UPDATE_VMEM = 48 * 1024 * 1024


def split(x):
    hi = x.astype(jnp.bfloat16)
    return hi, (x - hi.astype(jnp.float32)).astype(jnp.bfloat16)


def dot3(a_hi, a_lo, b_hi, b_lo):
    dot = functools.partial(jnp.dot, preferred_element_type=jnp.float32)
    return dot(a_hi, b_hi) + (dot(a_hi, b_lo) + dot(a_lo, b_hi))


def scale_kernel(place, *refs):
    parts, cores, (hi, lo) = refs[:4], refs[4], refs[-2:]
    group = jnp.concatenate([part[...] for part in parts], axis=0)
    scaled = dot3(*split(cores[...]), *split(group))
    hi[...], lo[...] = split(scaled.T)


def scale_into(place, parts, cores, previous, depth):
    width = parts[0][0].shape[1]
    rows = cores.shape[0]
    half = rows // 4
    tile = min(width, 1024)
    block = pl.BlockSpec((tile, rows), lambda i, place: (i, place[0]))
    shape = jax.ShapeDtypeStruct((width, depth), jnp.bfloat16)
    held = [] if previous is None else list(previous)
    return pl.pallas_call(
        scale_kernel,
        grid_spec=pltpu.PrefetchScalarGridSpec(
            num_scalar_prefetch=1,
            grid=(width // tile,),
            in_specs=[
                pl.BlockSpec((half, tile), functools.partial(lambda at, i, place: (at, i), at))
                for _, at in parts
            ]
            + [pl.BlockSpec((rows, rows), lambda i, place: (0, 0))]
            + [pl.BlockSpec(memory_space=pl.ANY)] * len(held),
            out_specs=[block, block],
        ),
        out_shape=[shape, shape],
        input_output_aliases={} if previous is None else {6: 0, 7: 1},
        compiler_params=pltpu.CompilerParams(vmem_limit_bytes=SCALE_VMEM),
    )(place, *(a for a, _ in parts), cores, *held)


def lay_kernel(planes, plane, *refs):
    sources, out, sems = refs[: 2 * planes - 1], refs[-2], refs[-1]
    blocks = out.shape[0] // planes
    for z in range(planes):

        @pl.when(plane[0] == z)
        def _():
            copies = [
                pltpu.make_async_copy(
                    sources[planes - 1 + q - z], out.at[pl.ds(q * blocks, blocks)], sems.at[q]
                )
                for q in range(planes)
            ]
            for copy in copies:
                copy.start()
            for copy in copies:
                copy.wait()


def lay(plane, sources):
    planes = (len(sources) + 1) // 2
    shape = sources[0].shape
    return pl.pallas_call(
        functools.partial(lay_kernel, planes),
        grid_spec=pltpu.PrefetchScalarGridSpec(
            num_scalar_prefetch=1,
            grid=(1,),
            in_specs=[pl.BlockSpec(memory_space=pl.ANY)] * len(sources),
            out_specs=pl.BlockSpec(memory_space=pl.ANY),
            scratch_shapes=[pltpu.SemaphoreType.DMA((planes,))],
        ),
        out_shape=jax.ShapeDtypeStruct((planes * shape[0], *shape[1:]), jnp.float32),
    )(plane, *sources)


def update_kernel(trailing, hi, lo, right, *refs):
    out, right_hi, right_lo = refs[-3:]

    @pl.when(pl.program_id(0) == 0)
    def _():
        right_hi[...], right_lo[...] = split(right[...])

    out[...] = trailing[...] - dot3(hi[...], lo[...], right_hi[...], right_lo[...])


def update_chunk(start, trailing, left, right, previous):
    height = trailing.shape[0]
    depth, wide = right.shape
    tile = min(height, 512)
    here = pl.BlockSpec((tile, wide), lambda i: (i, start // wide))
    side = pl.BlockSpec((tile, depth), lambda i: (i, 0))
    held = [] if previous is None else [previous]
    return pl.pallas_call(
        update_kernel,
        grid=(height // tile,),
        in_specs=[here, side, side, pl.BlockSpec((depth, wide), lambda i: (0, 0))]
        + [pl.BlockSpec(memory_space=pl.ANY)] * len(held),
        out_specs=here,
        out_shape=jax.ShapeDtypeStruct(trailing.shape, jnp.float32),
        scratch_shapes=[pltpu.VMEM((depth, wide), jnp.bfloat16)] * 2,
        input_output_aliases={} if previous is None else {4: 0},
        compiler_params=pltpu.CompilerParams(vmem_limit_bytes=UPDATE_VMEM),
    )(trailing, *left, right, *held)


def body(planes, columns, trailing, panel_factors, vectors_t, inverse_lower_factors, slot_of_panel):
    lines = columns // 2
    per_col, rank, _ = vectors_t.shape
    panels = per_col * columns
    rows = panel_factors.shape[0]
    width = trailing.shape[1]
    depth = rows * columns
    halves = columns // planes
    col = lax.axis_index("col")
    line, core = col // 2, col % 2

    def across(x, bits):
        return lax.ppermute(x, "col", [(i, i ^ bits) for i in range(columns)])

    def along(x, moves):
        return lax.ppermute(x, "row", moves)

    def column_chunk(number, source):
        at, wide = (eighths * width // 8 for eighths in CHUNKS[number])
        parts = [source[:, h * width + at : h * width + at + wide] for h in range(halves)]
        return at, jnp.stack(parts)

    after = lax.optimization_barrier

    starts, everywhere = [0], [None]
    for number in range(1, len(CHUNKS)):
        at, mine = column_chunk(number, panel_factors)
        starts.append(at)
        everywhere.append(lax.all_gather(mine, "row", axis=0, tiled=True))
    starts[0], mine = column_chunk(0, panel_factors)
    from_above, from_below = [mine], [mine]

    def hop(d):
        from_above.append(along(from_above[-1], [(p, p - 1) for p in range(1, planes - d + 1)]))
        from_below.append(along(from_below[-1], [(p, p + 1) for p in range(d - 1, planes - 1)]))

    cut = rows // 2
    own = [panel_factors[:cut], panel_factors[cut:]]
    gathered = [[own, None]] + [[None, None] for _ in range(lines - 1)]
    single = [1 << i for i in range(lines.bit_length() - 1)]
    for s in single:
        gathered[s][0] = [across(x, 2 * s) for x in own]
    for d in range(1, planes - 1):
        hop(d)

    arrived, hopped, vectors_t, inverse_lower_factors = after(
        (
            [gathered[s][0] for s in single],
            (from_above[-1], from_below[-1]),
            vectors_t,
            inverse_lower_factors,
        )
    )
    from_above[-1], from_below[-1] = hopped
    for s, x in zip(single, arrived):
        gathered[s][0] = x
    for s in sorted(range(1, lines), key=lambda s: bin(s).count("1")):
        low, high = s & -s, 1 << (s.bit_length() - 1)
        if low != high:
            gathered[s][0] = [
                across(gathered[s ^ high][0][0], 2 * high),
                across(gathered[s ^ low][0][1], 2 * low),
            ]
    solved = lax.dot_general(
        vectors_t, inverse_lower_factors, (((2,), (2,)), ((0,), (0,))), precision=HIGHEST
    )
    cores = jnp.einsum("fdv,fpv->fdp", solved, solved, precision=HIGHEST)
    bit = 1
    while bit < planes:
        cores = cores + along(cores, [(i, i ^ bit) for i in range(planes)])
        bit *= 2
    (from_above[-1], from_below[-1]), cores = after(((from_above[-1], from_below[-1]), cores))
    hop(planes - 1)

    far_lines = [s for s in range(1, lines) if s not in single]
    arrived, cores = after(([gathered[s][0] for s in far_lines], cores))
    for s, x in zip(far_lines, arrived):
        gathered[s][0] = x
    near = [cores] + [across(cores, 2 * s) for s in range(1, lines)]
    far = across(jnp.concatenate(near), 1)
    cores = jnp.concatenate(near + [far])
    gathered[0][1] = [across(panel_factors, 1)]
    for s in range(1, lines):
        gathered[s][1] = [across(x, 1) for x in gathered[s][0]]
    gathered[0][0] = [panel_factors]

    plane = lax.axis_index("row").astype(jnp.int32).reshape(1)
    everywhere[0] = lay(plane, from_below[:0:-1] + [mine] + from_above[1:])
    everywhere[0], cores = after((everywhere[0], cores))

    def exchange(number):
        chunk = lax.all_to_all(everywhere[number], "col", split_axis=0, concat_axis=0, tiled=True)
        return chunk.reshape(depth, -1)

    chunks = [exchange(0)]

    owner = col ^ jnp.arange(columns, dtype=jnp.int32)
    panel = (owner[:, None] * per_col + jnp.arange(per_col, dtype=jnp.int32)[None, :]).reshape(panels)
    slot = slot_of_panel[panel]
    holder = slot // per_col ^ col
    panel_cores = cores[(holder % 2 * lines + holder // 2) * per_col + slot % per_col]
    together = 2 * per_col
    diagonal = jnp.eye(together, dtype=jnp.float32)
    blocks = (
        panel_cores.reshape(lines, together, rank, 1, rank) * diagonal[None, :, None, :, None]
    ).reshape(lines, together * rank, together * rank)
    blocks = jnp.where(core == 0, blocks, jnp.roll(blocks, rows, axis=1))

    left = None
    for s in range(lines):
        place = (line ^ s).astype(jnp.int32).reshape(1)
        parts = []
        for group in gathered[s]:
            parts += [(group[0], 0), (group[0], 1)] if len(group) == 1 else [(x, 0) for x in group]
        left = scale_into(place, parts, blocks[s], left, depth)

    everywhere[1], left = after((everywhere[1], left))
    chunks.append(exchange(1))
    updated = None
    for number, start in enumerate(starts):
        updated = update_chunk(start, trailing, left, chunks[number], updated)
        if number + 2 < len(starts):
            everywhere[number + 2], updated = after((everywhere[number + 2], updated))
            chunks.append(exchange(number + 2))
    return updated


def solution(mesh):
    planes, columns = mesh.shape["row"], mesh.shape["col"]
    if columns != 2 * planes or planes & (planes - 1):
        raise ValueError("unsupported mesh")
    return jax.shard_map(
        functools.partial(body, planes, columns),
        mesh=mesh,
        in_specs=(
            P("row", "col"),
            P("col", "row"),
            P("col", None, None),
            P("col", "row", None),
            P(),
        ),
        out_specs=P("row", "col"),
        check_vma=False,
    )
```

```python
import functools

import jax
import jax.numpy as jnp
from jax import lax
from jax.experimental import pallas as pl
from jax.experimental.pallas import tpu as pltpu
from jax.sharding import PartitionSpec as P

CHUNKS = ((0, 2), (2, 2), (4, 2), (6, 2))
HIGHEST = lax.Precision.HIGHEST
SCALE_VMEM = 48 * 1024 * 1024
UPDATE_VMEM = 48 * 1024 * 1024
EARLY = pl.CostEstimate(flops=1, bytes_accessed=1, transcendentals=0)


def split(x):
    hi = x.astype(jnp.bfloat16)
    return hi, (x - hi.astype(jnp.float32)).astype(jnp.bfloat16)


def dot3(a_hi, a_lo, b_hi, b_lo):
    dot = functools.partial(jnp.dot, preferred_element_type=jnp.float32)
    return dot(a_hi, b_hi) + (dot(a_hi, b_lo) + dot(a_lo, b_hi))


def scale_kernel(place, *refs):
    parts, cores, (hi, lo) = refs[:4], refs[4], refs[-2:]
    group = jnp.concatenate([part[...] for part in parts], axis=0)
    scaled = dot3(*split(cores[...]), *split(group))
    hi[...], lo[...] = split(scaled.T)


def scale_into(place, parts, cores, previous, depth):
    width = parts[0][0].shape[1]
    rows = cores.shape[0]
    half = rows // 4
    tile = min(width, 1024)
    block = pl.BlockSpec((tile, rows), lambda i, place: (i, place[0]))
    shape = jax.ShapeDtypeStruct((width, depth), jnp.bfloat16)
    held = [] if previous is None else list(previous)
    return pl.pallas_call(
        scale_kernel,
        grid_spec=pltpu.PrefetchScalarGridSpec(
            num_scalar_prefetch=1,
            grid=(width // tile,),
            in_specs=[
                pl.BlockSpec((half, tile), functools.partial(lambda at, i, place: (at, i), at))
                for _, at in parts
            ]
            + [pl.BlockSpec((rows, rows), lambda i, place: (0, 0))]
            + [pl.BlockSpec(memory_space=pl.ANY)] * len(held),
            out_specs=[block, block],
        ),
        out_shape=[shape, shape],
        input_output_aliases={} if previous is None else {6: 0, 7: 1},
        compiler_params=pltpu.CompilerParams(vmem_limit_bytes=SCALE_VMEM),
        cost_estimate=EARLY,
    )(place, *(a for a, _ in parts), cores, *held)


def lay_kernel(planes, plane, *refs):
    sources, out, sems = refs[: 2 * planes - 1], refs[-2], refs[-1]
    blocks = out.shape[0] // planes
    for z in range(planes):

        @pl.when(plane[0] == z)
        def _():
            copies = [
                pltpu.make_async_copy(
                    sources[planes - 1 + q - z], out.at[pl.ds(q * blocks, blocks)], sems.at[q]
                )
                for q in range(planes)
            ]
            for copy in copies:
                copy.start()
            for copy in copies:
                copy.wait()


def lay(plane, sources):
    planes = (len(sources) + 1) // 2
    shape = sources[0].shape
    return pl.pallas_call(
        functools.partial(lay_kernel, planes),
        grid_spec=pltpu.PrefetchScalarGridSpec(
            num_scalar_prefetch=1,
            grid=(1,),
            in_specs=[pl.BlockSpec(memory_space=pl.ANY)] * len(sources),
            out_specs=pl.BlockSpec((planes * shape[0], *shape[1:]), lambda i, plane: (0, 0, 0)),
            scratch_shapes=[pltpu.SemaphoreType.DMA((planes,))],
        ),
        out_shape=jax.ShapeDtypeStruct((planes * shape[0], *shape[1:]), jnp.float32),
        compiler_params=pltpu.CompilerParams(vmem_limit_bytes=SCALE_VMEM),
        cost_estimate=EARLY,
    )(plane, *sources)


def update_kernel(trailing, hi, lo, right, *refs):
    out, right_hi, right_lo = refs[-3:]

    @pl.when(pl.program_id(0) == 0)
    def _():
        right_hi[...], right_lo[...] = split(right[...])

    out[...] = trailing[...] - dot3(hi[...], lo[...], right_hi[...], right_lo[...])


def update_chunk(start, trailing, left, right, previous):
    height = trailing.shape[0]
    depth, wide = right.shape
    tile = min(height, 512)
    here = pl.BlockSpec((tile, wide), lambda i: (i, start // wide))
    side = pl.BlockSpec((tile, depth), lambda i: (i, 0))
    held = [] if previous is None else [previous]
    return pl.pallas_call(
        update_kernel,
        grid=(height // tile,),
        in_specs=[here, side, side, pl.BlockSpec((depth, wide), lambda i: (0, 0))]
        + [pl.BlockSpec(memory_space=pl.ANY)] * len(held),
        out_specs=here,
        out_shape=jax.ShapeDtypeStruct(trailing.shape, jnp.float32),
        scratch_shapes=[pltpu.VMEM((depth, wide), jnp.bfloat16)] * 2,
        input_output_aliases={} if previous is None else {4: 0},
        compiler_params=pltpu.CompilerParams(vmem_limit_bytes=UPDATE_VMEM),
        cost_estimate=EARLY,
    )(trailing, *left, right, *held)


def body(planes, columns, trailing, panel_factors, vectors_t, inverse_lower_factors, slot_of_panel):
    lines = columns // 2
    per_col, rank, _ = vectors_t.shape
    panels = per_col * columns
    rows = panel_factors.shape[0]
    width = trailing.shape[1]
    depth = rows * columns
    halves = columns // planes
    col = lax.axis_index("col")
    line, core = col // 2, col % 2

    def across(x, bits):
        return lax.ppermute(x, "col", [(i, i ^ bits) for i in range(columns)])

    def along(x, moves):
        return lax.ppermute(x, "row", moves)

    def column_chunk(number, source):
        at, wide = (eighths * width // 8 for eighths in CHUNKS[number])
        parts = [source[:, h * width + at : h * width + at + wide] for h in range(halves)]
        return at, jnp.stack(parts)

    after = lax.optimization_barrier

    starts, everywhere = [0], [None]
    for number in range(1, len(CHUNKS)):
        at, mine = column_chunk(number, panel_factors)
        starts.append(at)
        everywhere.append(lax.all_gather(mine, "row", axis=0, tiled=True))
    starts[0], mine = column_chunk(0, panel_factors)
    from_above, from_below = [mine], [mine]

    def hop(d):
        from_above.append(along(from_above[-1], [(p, p - 1) for p in range(1, planes - d + 1)]))
        from_below.append(along(from_below[-1], [(p, p + 1) for p in range(d - 1, planes - 1)]))

    cut = rows // 2
    own = [panel_factors[:cut], panel_factors[cut:]]
    gathered = [[own, None]] + [[None, None] for _ in range(lines - 1)]
    single = [1 << i for i in range(lines.bit_length() - 1)]
    for s in single:
        gathered[s][0] = [across(x, 2 * s) for x in own]
    hop(1)

    arrived, hopped, vectors_t, inverse_lower_factors = after(
        (
            [gathered[s][0] for s in single],
            (from_above[-1], from_below[-1]),
            vectors_t,
            inverse_lower_factors,
        )
    )
    from_above[-1], from_below[-1] = hopped
    for s, x in zip(single, arrived):
        gathered[s][0] = x
    for s in sorted(range(1, lines), key=lambda s: bin(s).count("1")):
        low, high = s & -s, 1 << (s.bit_length() - 1)
        if low != high:
            gathered[s][0] = [
                across(gathered[s ^ high][0][0], 2 * high),
                across(gathered[s ^ low][0][1], 2 * low),
            ]
    solved = lax.dot_general(
        vectors_t, inverse_lower_factors, (((2,), (2,)), ((0,), (0,))), precision=HIGHEST
    )
    cores = jnp.einsum("fdv,fpv->fdp", solved, solved, precision=HIGHEST)
    bit = 1
    while bit < planes:
        cores = cores + along(cores, [(i, i ^ bit) for i in range(planes)])
        bit *= 2
    hop(2)

    far_lines = [s for s in range(1, lines) if s not in single]
    arrived, hopped, cores, everywhere[1] = after(
        ([gathered[s][0] for s in far_lines], (from_above[-1], from_below[-1]), cores, everywhere[1])
    )
    from_above[-1], from_below[-1] = hopped
    for d in range(3, planes):
        hop(d)
    for s, x in zip(far_lines, arrived):
        gathered[s][0] = x
    near = [cores] + [across(cores, 2 * s) for s in range(1, lines)]
    far = across(jnp.concatenate(near), 1)
    cores = jnp.concatenate(near + [far])
    gathered[0][1] = [across(panel_factors, 1)]
    for s in range(1, lines):
        gathered[s][1] = [across(x, 1) for x in gathered[s][0]]
    gathered[0][0] = [panel_factors]

    def exchange(number):
        chunk = lax.all_to_all(everywhere[number], "col", split_axis=0, concat_axis=0, tiled=True)
        return chunk.reshape(depth, -1)

    chunks = {1: exchange(1)}

    owner = col ^ jnp.arange(columns, dtype=jnp.int32)
    panel = (owner[:, None] * per_col + jnp.arange(per_col, dtype=jnp.int32)[None, :]).reshape(panels)
    slot = slot_of_panel[panel]
    holder = slot // per_col ^ col
    panel_cores = cores[(holder % 2 * lines + holder // 2) * per_col + slot % per_col]
    together = 2 * per_col
    diagonal = jnp.eye(together, dtype=jnp.float32)
    blocks = (
        panel_cores.reshape(lines, together, rank, 1, rank) * diagonal[None, :, None, :, None]
    ).reshape(lines, together * rank, together * rank)
    blocks = jnp.where(core == 0, blocks, jnp.roll(blocks, rows, axis=1))

    left = None
    for s in range(lines):
        place = (line ^ s).astype(jnp.int32).reshape(1)
        parts = []
        for group in gathered[s]:
            parts += [(group[0], 0), (group[0], 1)] if len(group) == 1 else [(x, 0) for x in group]
        left = scale_into(place, parts, blocks[s], left, depth)

    plane = lax.axis_index("row").astype(jnp.int32).reshape(1)
    everywhere[0] = lay(plane, from_below[:0:-1] + [mine] + from_above[1:])
    everywhere[0], left = after((everywhere[0], left))
    chunks[0] = exchange(0)
    updated = None
    order = [1, 0] + list(range(2, len(CHUNKS)))
    for at, number in enumerate(order):
        updated = update_chunk(starts[number], trailing, left, chunks[number], updated)
        if at + 2 < len(order):
            later = order[at + 2]
            everywhere[later], updated = after((everywhere[later], updated))
            chunks[later] = exchange(later)
    return updated


def solution(mesh):
    planes, columns = mesh.shape["row"], mesh.shape["col"]
    if columns != 2 * planes or planes & (planes - 1):
        raise ValueError("unsupported mesh")
    return jax.shard_map(
        functools.partial(body, planes, columns),
        mesh=mesh,
        in_specs=(
            P("row", "col"),
            P("col", "row"),
            P("col", None, None),
            P("col", "row", None),
            P(),
        ),
        out_specs=P("row", "col"),
        check_vma=False,
    )
```

```python
import functools

import jax
import jax.numpy as jnp
from jax import lax
from jax.experimental import pallas as pl
from jax.experimental.pallas import tpu as pltpu
from jax.sharding import PartitionSpec as P

HOPPED = (6, 2)
GATHERED = ((0, 3), (3, 3))
ORDER = ((1, 0, 3), (0, 6, 2), (2, 4, 2), (2, 3, 1))
HIGHEST = lax.Precision.HIGHEST
SCALE_VMEM = 48 * 1024 * 1024
UPDATE_VMEM = 48 * 1024 * 1024
EARLY = pl.CostEstimate(flops=1, bytes_accessed=1, transcendentals=0)


def split(x):
    hi = x.astype(jnp.bfloat16)
    return hi, (x - hi.astype(jnp.float32)).astype(jnp.bfloat16)


def dot3(a_hi, a_lo, b_hi, b_lo):
    dot = functools.partial(jnp.dot, preferred_element_type=jnp.float32)
    return dot(a_hi, b_hi) + (dot(a_hi, b_lo) + dot(a_lo, b_hi))


def scale_kernel(place, *refs):
    parts, cores, (hi, lo) = refs[:4], refs[4], refs[-2:]
    group = jnp.concatenate([part[...] for part in parts], axis=0)
    scaled = dot3(*split(cores[...]), *split(group))
    hi[...], lo[...] = split(scaled.T)


def scale_into(place, parts, cores, previous, depth):
    width = parts[0][0].shape[1]
    rows = cores.shape[0]
    half = rows // 4
    tile = min(width, 1024)
    block = pl.BlockSpec((tile, rows), lambda i, place: (i, place[0]))
    shape = jax.ShapeDtypeStruct((width, depth), jnp.bfloat16)
    held = [] if previous is None else list(previous)
    return pl.pallas_call(
        scale_kernel,
        grid_spec=pltpu.PrefetchScalarGridSpec(
            num_scalar_prefetch=1,
            grid=(width // tile,),
            in_specs=[
                pl.BlockSpec((half, tile), functools.partial(lambda at, i, place: (at, i), at))
                for _, at in parts
            ]
            + [pl.BlockSpec((rows, rows), lambda i, place: (0, 0))]
            + [pl.BlockSpec(memory_space=pl.ANY)] * len(held),
            out_specs=[block, block],
        ),
        out_shape=[shape, shape],
        input_output_aliases={} if previous is None else {6: 0, 7: 1},
        compiler_params=pltpu.CompilerParams(vmem_limit_bytes=SCALE_VMEM),
        cost_estimate=EARLY,
    )(place, *(a for a, _ in parts), cores, *held)


def lay_kernel(planes, plane, *refs):
    sources, out, sems = refs[: 2 * planes - 1], refs[-2], refs[-1]
    blocks = out.shape[0] // planes
    for z in range(planes):

        @pl.when(plane[0] == z)
        def _():
            copies = [
                pltpu.make_async_copy(
                    sources[planes - 1 + q - z], out.at[pl.ds(q * blocks, blocks)], sems.at[q]
                )
                for q in range(planes)
            ]
            for copy in copies:
                copy.start()
            for copy in copies:
                copy.wait()


def lay(plane, sources):
    planes = (len(sources) + 1) // 2
    shape = sources[0].shape
    return pl.pallas_call(
        functools.partial(lay_kernel, planes),
        grid_spec=pltpu.PrefetchScalarGridSpec(
            num_scalar_prefetch=1,
            grid=(1,),
            in_specs=[pl.BlockSpec(memory_space=pl.ANY)] * len(sources),
            out_specs=pl.BlockSpec((planes * shape[0], *shape[1:]), lambda i, plane: (0, 0, 0)),
            scratch_shapes=[pltpu.SemaphoreType.DMA((planes,))],
        ),
        out_shape=jax.ShapeDtypeStruct((planes * shape[0], *shape[1:]), jnp.float32),
        compiler_params=pltpu.CompilerParams(vmem_limit_bytes=SCALE_VMEM),
        cost_estimate=EARLY,
    )(plane, *sources)


def update_kernel(trailing, hi, lo, right, *refs):
    out, right_hi, right_lo = refs[-3:]

    @pl.when(pl.program_id(0) == 0)
    def _():
        right_hi[...], right_lo[...] = split(right[...])

    out[...] = trailing[...] - dot3(hi[...], lo[...], right_hi[...], right_lo[...])


def update_chunk(start, trailing, left, right, previous):
    height = trailing.shape[0]
    depth, wide = right.shape
    tile = min(height, 512)
    here = pl.BlockSpec((tile, wide), lambda i: (i, start // wide))
    side = pl.BlockSpec((tile, depth), lambda i: (i, 0))
    held = [] if previous is None else [previous]
    return pl.pallas_call(
        update_kernel,
        grid=(height // tile,),
        in_specs=[here, side, side, pl.BlockSpec((depth, wide), lambda i: (0, 0))]
        + [pl.BlockSpec(memory_space=pl.ANY)] * len(held),
        out_specs=here,
        out_shape=jax.ShapeDtypeStruct(trailing.shape, jnp.float32),
        scratch_shapes=[pltpu.VMEM((depth, wide), jnp.bfloat16)] * 2,
        input_output_aliases={} if previous is None else {4: 0},
        compiler_params=pltpu.CompilerParams(vmem_limit_bytes=UPDATE_VMEM),
        cost_estimate=EARLY,
    )(trailing, *left, right, *held)


def body(planes, columns, trailing, panel_factors, vectors_t, inverse_lower_factors, slot_of_panel):
    lines = columns // 2
    per_col, rank, _ = vectors_t.shape
    panels = per_col * columns
    rows = panel_factors.shape[0]
    width = trailing.shape[1]
    depth = rows * columns
    halves = columns // planes
    col = lax.axis_index("col")
    line, core = col // 2, col % 2

    def across(x, bits):
        return lax.ppermute(x, "col", [(i, i ^ bits) for i in range(columns)])

    def along(x, moves):
        return lax.ppermute(x, "row", moves)

    eighth = width // 8

    def column_chunk(first, count):
        parts = []
        for h in range(halves):
            at = h * width + first * eighth
            parts.append(panel_factors[:, at : at + count * eighth])
        return jnp.stack(parts)

    after = lax.optimization_barrier

    everywhere = [None] + [
        lax.all_gather(column_chunk(*columns_of), "row", axis=0, tiled=True) for columns_of in GATHERED
    ]
    solved = lax.dot_general(
        vectors_t, inverse_lower_factors, (((2,), (2,)), ((0,), (0,))), precision=HIGHEST
    )
    cores = jnp.einsum("fdv,fpv->fdp", solved, solved, precision=HIGHEST)
    bit = 1
    while bit < planes:
        cores = cores + along(cores, [(i, i ^ bit) for i in range(planes)])
        bit *= 2
    mine, cores = after((column_chunk(*HOPPED), cores))
    from_above, from_below = [mine], [mine]

    def hop(d):
        from_above.append(along(from_above[-1], [(p, p - 1) for p in range(1, planes - d + 1)]))
        from_below.append(along(from_below[-1], [(p, p + 1) for p in range(d - 1, planes - 1)]))

    cut = rows // 2
    own = [panel_factors[:cut], panel_factors[cut:]]
    gathered = [[own, None]] + [[None, None] for _ in range(lines - 1)]
    single = [1 << i for i in range(lines.bit_length() - 1)]
    for s in single:
        gathered[s][0] = [across(x, 2 * s) for x in own]
    hop(1)

    arrived, hopped, cores = after(
        ([gathered[s][0] for s in single], (from_above[-1], from_below[-1]), cores)
    )
    from_above[-1], from_below[-1] = hopped
    for s, x in zip(single, arrived):
        gathered[s][0] = x
    for s in sorted(range(1, lines), key=lambda s: bin(s).count("1")):
        low, high = s & -s, 1 << (s.bit_length() - 1)
        if low != high:
            gathered[s][0] = [
                across(gathered[s ^ high][0][0], 2 * high),
                across(gathered[s ^ low][0][1], 2 * low),
            ]
    near = [cores] + [across(cores, 2 * s) for s in range(1, lines)]
    hop(2)

    far_lines = [s for s in range(1, lines) if s not in single]
    arrived, hopped, near, everywhere[1] = after(
        ([gathered[s][0] for s in far_lines], (from_above[-1], from_below[-1]), near, everywhere[1])
    )
    from_above[-1], from_below[-1] = hopped
    for d in range(3, planes):
        hop(d)
    for s, x in zip(far_lines, arrived):
        gathered[s][0] = x
    far = across(jnp.concatenate(near), 1)
    cores = jnp.concatenate(near + [far])
    gathered[0][1] = [across(panel_factors, 1)]
    for s in range(1, lines):
        gathered[s][1] = [across(x, 1) for x in gathered[s][0]]
    gathered[0][0] = [panel_factors]

    def exchange(number):
        source, first, count = ORDER[number]
        sent = everywhere[source]
        if source and GATHERED[source - 1][1] != count:
            at = (first - GATHERED[source - 1][0]) * eighth
            sent = sent[:, :, at : at + count * eighth]
        chunk = lax.all_to_all(sent, "col", split_axis=0, concat_axis=0, tiled=True)
        return chunk.reshape(depth, -1)

    chunks = [exchange(0)]

    owner = col ^ jnp.arange(columns, dtype=jnp.int32)
    panel = (owner[:, None] * per_col + jnp.arange(per_col, dtype=jnp.int32)[None, :]).reshape(panels)
    slot = slot_of_panel[panel]
    holder = slot // per_col ^ col
    panel_cores = cores[(holder % 2 * lines + holder // 2) * per_col + slot % per_col]
    together = 2 * per_col
    diagonal = jnp.eye(together, dtype=jnp.float32)
    blocks = (
        panel_cores.reshape(lines, together, rank, 1, rank) * diagonal[None, :, None, :, None]
    ).reshape(lines, together * rank, together * rank)
    blocks = jnp.where(core == 0, blocks, jnp.roll(blocks, rows, axis=1))

    left = None
    for s in range(lines):
        place = (line ^ s).astype(jnp.int32).reshape(1)
        parts = []
        for group in gathered[s]:
            parts += [(group[0], 0), (group[0], 1)] if len(group) == 1 else [(x, 0) for x in group]
        left = scale_into(place, parts, blocks[s], left, depth)

    plane = lax.axis_index("row").astype(jnp.int32).reshape(1)
    everywhere[0] = lay(plane, from_below[:0:-1] + [mine] + from_above[1:])
    everywhere[0], left = after((everywhere[0], left))
    chunks.append(exchange(1))
    updated = None
    for number, (_, first, _) in enumerate(ORDER):
        updated = update_chunk(first * eighth, trailing, left, chunks[number], updated)
        if number + 2 < len(ORDER):
            source = ORDER[number + 2][0]
            everywhere[source], updated = after((everywhere[source], updated))
            chunks.append(exchange(number + 2))
    return updated


def solution(mesh):
    planes, columns = mesh.shape["row"], mesh.shape["col"]
    if columns != 2 * planes or planes & (planes - 1):
        raise ValueError("unsupported mesh")
    return jax.shard_map(
        functools.partial(body, planes, columns),
        mesh=mesh,
        in_specs=(
            P("row", "col"),
            P("col", "row"),
            P("col", None, None),
            P("col", "row", None),
            P(),
        ),
        out_specs=P("row", "col"),
        check_vma=False,
    )
```

```python
import functools

import jax
import jax.numpy as jnp
from jax import lax
from jax.experimental import pallas as pl
from jax.experimental.pallas import tpu as pltpu
from jax.sharding import PartitionSpec as P

HOPPED = (6, 2)
GATHERED = ((0, 3), (3, 3))
ORDER = ((1, 0, 3), (0, 6, 2), (2, 4, 2), (2, 3, 1))
HIGHEST = lax.Precision.HIGHEST
SCALE_VMEM = 48 * 1024 * 1024
UPDATE_VMEM = 48 * 1024 * 1024
EARLY = pl.CostEstimate(flops=1, bytes_accessed=1, transcendentals=0)


def split(x):
    hi = x.astype(jnp.bfloat16)
    return hi, (x - hi.astype(jnp.float32)).astype(jnp.bfloat16)


def dot3(a_hi, a_lo, b_hi, b_lo):
    dot = functools.partial(jnp.dot, preferred_element_type=jnp.float32)
    return dot(a_hi, b_hi) + (dot(a_hi, b_lo) + dot(a_lo, b_hi))


def scale_kernel(place, *refs):
    parts, cores, (hi, lo) = refs[:4], refs[4], refs[-2:]
    group = jnp.concatenate([part[...] for part in parts], axis=0)
    scaled = dot3(*split(cores[0]), *split(group))
    hi[...], lo[...] = split(scaled.T)


def scale_into(place, parts, cores, line, previous, depth):
    width = parts[0][0].shape[1]
    rows = cores.shape[1]
    half = rows // 4
    tile = min(width, 1024)
    block = pl.BlockSpec((tile, rows), lambda i, place: (i, place[0]))
    shape = jax.ShapeDtypeStruct((width, depth), jnp.bfloat16)
    held = [] if previous is None else list(previous)
    return pl.pallas_call(
        scale_kernel,
        grid_spec=pltpu.PrefetchScalarGridSpec(
            num_scalar_prefetch=1,
            grid=(width // tile,),
            in_specs=[
                pl.BlockSpec((half, tile), functools.partial(lambda at, i, place: (at, i), at))
                for _, at in parts
            ]
            + [pl.BlockSpec((1, rows, rows), lambda i, place: (line, 0, 0))]
            + [pl.BlockSpec(memory_space=pl.ANY)] * len(held),
            out_specs=[block, block],
        ),
        out_shape=[shape, shape],
        input_output_aliases={} if previous is None else {6: 0, 7: 1},
        compiler_params=pltpu.CompilerParams(vmem_limit_bytes=SCALE_VMEM),
        cost_estimate=EARLY,
    )(place, *(a for a, _ in parts), cores, *held)


def blocks_kernel(per_col, col, slots, *refs):
    near, far, (out, held) = refs[:-3], refs[-3], refs[-2:]
    lines = len(near)
    rank = held.shape[1]
    together = 2 * per_col
    for s in range(lines):
        held[s * together : s * together + per_col] = near[s][...]
        held[s * together + per_col : (s + 1) * together] = far[s * per_col : (s + 1) * per_col]
    out[...] = jnp.zeros_like(out)
    me = col[0]
    for s in range(lines):
        for t in range(together):
            owner = me ^ (2 * s + t // per_col)
            slot = slots[owner * per_col + t % per_col]
            block = held[((slot // per_col) ^ me) * per_col + slot % per_col]
            row = (t + (me % 2) * per_col) % together
            out[s, pl.ds(pl.multiple_of(row * rank, rank), rank), t * rank : (t + 1) * rank] = block


def diagonal_blocks(col, slots, near, far):
    per_col, rank, _ = near[0].shape
    lines = len(near)
    size = 2 * per_col * rank
    return pl.pallas_call(
        functools.partial(blocks_kernel, per_col),
        grid_spec=pltpu.PrefetchScalarGridSpec(
            num_scalar_prefetch=2,
            grid=(1,),
            in_specs=[pl.BlockSpec(x.shape, lambda i, col, slots: (0, 0, 0)) for x in (*near, far)],
            out_specs=pl.BlockSpec((lines, size, size), lambda i, col, slots: (0, 0, 0)),
            scratch_shapes=[pltpu.VMEM((2 * lines * per_col, rank, rank), jnp.float32)],
        ),
        out_shape=jax.ShapeDtypeStruct((lines, size, size), jnp.float32),
        compiler_params=pltpu.CompilerParams(vmem_limit_bytes=SCALE_VMEM),
        cost_estimate=EARLY,
    )(col, slots, *near, far)


def lay_kernel(planes, plane, *refs):
    sources, out, sems = refs[: 2 * planes - 1], refs[-2], refs[-1]
    blocks = out.shape[0] // planes
    for z in range(planes):

        @pl.when(plane[0] == z)
        def _():
            copies = [
                pltpu.make_async_copy(
                    sources[planes - 1 + q - z], out.at[pl.ds(q * blocks, blocks)], sems.at[q]
                )
                for q in range(planes)
            ]
            for copy in copies:
                copy.start()
            for copy in copies:
                copy.wait()


def lay(plane, sources):
    planes = (len(sources) + 1) // 2
    shape = sources[0].shape
    return pl.pallas_call(
        functools.partial(lay_kernel, planes),
        grid_spec=pltpu.PrefetchScalarGridSpec(
            num_scalar_prefetch=1,
            grid=(1,),
            in_specs=[pl.BlockSpec(memory_space=pl.ANY)] * len(sources),
            out_specs=pl.BlockSpec((planes * shape[0], *shape[1:]), lambda i, plane: (0, 0, 0)),
            scratch_shapes=[pltpu.SemaphoreType.DMA((planes,))],
        ),
        out_shape=jax.ShapeDtypeStruct((planes * shape[0], *shape[1:]), jnp.float32),
        compiler_params=pltpu.CompilerParams(vmem_limit_bytes=SCALE_VMEM),
        cost_estimate=EARLY,
    )(plane, *sources)


def update_kernel(trailing, hi, lo, right, *refs):
    out, right_hi, right_lo = refs[-3:]

    @pl.when(pl.program_id(0) == 0)
    def _():
        right_hi[...], right_lo[...] = split(right[...])

    out[...] = trailing[...] - dot3(hi[...], lo[...], right_hi[...], right_lo[...])


def update_chunk(start, trailing, left, right, previous):
    height = trailing.shape[0]
    depth, wide = right.shape
    tile = min(height, 512)
    here = pl.BlockSpec((tile, wide), lambda i: (i, start // wide))
    side = pl.BlockSpec((tile, depth), lambda i: (i, 0))
    held = [] if previous is None else [previous]
    return pl.pallas_call(
        update_kernel,
        grid=(height // tile,),
        in_specs=[here, side, side, pl.BlockSpec((depth, wide), lambda i: (0, 0))]
        + [pl.BlockSpec(memory_space=pl.ANY)] * len(held),
        out_specs=here,
        out_shape=jax.ShapeDtypeStruct(trailing.shape, jnp.float32),
        scratch_shapes=[pltpu.VMEM((depth, wide), jnp.bfloat16)] * 2,
        input_output_aliases={} if previous is None else {4: 0},
        compiler_params=pltpu.CompilerParams(vmem_limit_bytes=UPDATE_VMEM),
        cost_estimate=EARLY,
    )(trailing, *left, right, *held)


def body(planes, columns, trailing, panel_factors, vectors_t, inverse_lower_factors, slot_of_panel):
    lines = columns // 2
    rows = panel_factors.shape[0]
    width = trailing.shape[1]
    depth = rows * columns
    halves = columns // planes
    col = lax.axis_index("col")
    line = col // 2

    def across(x, bits):
        return lax.ppermute(x, "col", [(i, i ^ bits) for i in range(columns)])

    def along(x, moves):
        return lax.ppermute(x, "row", moves)

    eighth = width // 8

    def column_chunk(first, count):
        parts = []
        for h in range(halves):
            at = h * width + first * eighth
            parts.append(panel_factors[:, at : at + count * eighth])
        return jnp.stack(parts)

    after = lax.optimization_barrier

    everywhere = [None] + [
        lax.all_gather(column_chunk(*columns_of), "row", axis=0, tiled=True) for columns_of in GATHERED
    ]
    solved = lax.dot_general(
        vectors_t, inverse_lower_factors, (((2,), (2,)), ((0,), (0,))), precision=HIGHEST
    )
    cores = jnp.einsum("fdv,fpv->fdp", solved, solved, precision=HIGHEST)
    bit = 1
    while bit < planes:
        cores = cores + along(cores, [(i, i ^ bit) for i in range(planes)])
        bit *= 2
    bulk, cores = after((panel_factors, cores))
    near = [cores] + [across(cores, 2 * s) for s in range(1, lines)]

    cut = rows // 2
    gathered = [[[bulk], None]] + [[None, None] for _ in range(lines - 1)]
    single = [1 << i for i in range(lines.bit_length() - 1)]
    for s in single:
        gathered[s][0] = [across(bulk, 2 * s)]

    mine, near = after((column_chunk(*HOPPED), near))
    from_above, from_below = [mine], [mine]

    def hop(d):
        from_above.append(along(from_above[-1], [(p, p - 1) for p in range(1, planes - d + 1)]))
        from_below.append(along(from_below[-1], [(p, p + 1) for p in range(d - 1, planes - 1)]))

    hop(1)
    far = across(jnp.concatenate(near), 1)
    gathered[0][1] = [across(bulk, 1)]

    arrived, hopped, far, gathered[0][1] = after(
        ([gathered[s][0] for s in single], (from_above[-1], from_below[-1]), far, gathered[0][1])
    )
    from_above[-1], from_below[-1] = hopped
    for s, x in zip(single, arrived):
        gathered[s][0] = x
    several = sorted((s for s in range(1, lines) if s not in single), key=lambda s: bin(s).count("1"))
    for s in several:
        low, high = s & -s, 1 << (s.bit_length() - 1)
        upper, lower = gathered[s ^ high][0], gathered[s ^ low][0]
        gathered[s][0] = [
            across(upper[0][:cut], 2 * high),
            across(lower[-1][-cut:], 2 * low),
        ]
    hop(2)
    for s in single:
        gathered[s][1] = [across(x, 1) for x in gathered[s][0]]

    arrived, hopped, swapped, everywhere[1] = after(
        (
            [gathered[s][0] for s in several],
            (from_above[-1], from_below[-1]),
            [gathered[s][1] for s in single],
            everywhere[1],
        )
    )
    from_above[-1], from_below[-1] = hopped
    for s, x in zip(several, arrived):
        gathered[s][0] = x
        gathered[s][1] = [across(part, 1) for part in x]
    for s, x in zip(single, swapped):
        gathered[s][1] = x
    for d in range(3, planes):
        hop(d)

    def exchange(number):
        source, first, count = ORDER[number]
        sent = everywhere[source]
        if source and GATHERED[source - 1][1] != count:
            at = (first - GATHERED[source - 1][0]) * eighth
            sent = sent[:, :, at : at + count * eighth]
        chunk = lax.all_to_all(sent, "col", split_axis=0, concat_axis=0, tiled=True)
        return chunk.reshape(depth, -1)

    chunks = [exchange(0)]
    blocks = diagonal_blocks(col.astype(jnp.int32).reshape(1), slot_of_panel, near, far)

    left = None
    for s in range(lines):
        place = (line ^ s).astype(jnp.int32).reshape(1)
        parts = []
        for group in gathered[s]:
            parts += [(group[0], 0), (group[0], 1)] if len(group) == 1 else [(x, 0) for x in group]
        left = scale_into(place, parts, blocks, s, left, depth)

    plane = lax.axis_index("row").astype(jnp.int32).reshape(1)
    everywhere[0] = lay(plane, from_below[:0:-1] + [mine] + from_above[1:])
    everywhere[0], left = after((everywhere[0], left))
    chunks.append(exchange(1))
    updated = None
    for number, (_, first, _) in enumerate(ORDER):
        updated = update_chunk(first * eighth, trailing, left, chunks[number], updated)
        if number + 2 < len(ORDER):
            source = ORDER[number + 2][0]
            everywhere[source], updated = after((everywhere[source], updated))
            chunks.append(exchange(number + 2))
    return updated


def solution(mesh):
    planes, columns = mesh.shape["row"], mesh.shape["col"]
    if columns != 2 * planes or planes & (planes - 1):
        raise ValueError("unsupported mesh")
    return jax.shard_map(
        functools.partial(body, planes, columns),
        mesh=mesh,
        in_specs=(
            P("row", "col"),
            P("col", "row"),
            P("col", None, None),
            P("col", "row", None),
            P(),
        ),
        out_specs=P("row", "col"),
        check_vma=False,
    )
```

```python
import functools

import jax
import jax.numpy as jnp
from jax import lax
from jax.experimental import pallas as pl
from jax.experimental.pallas import tpu as pltpu
from jax.sharding import PartitionSpec as P

CHUNKS = ((0, 4), (4, 2), (6, 2))
HIGHEST = lax.Precision.HIGHEST
SCALE_VMEM = 48 * 1024 * 1024
UPDATE_VMEM = 48 * 1024 * 1024
EARLY = pl.CostEstimate(flops=1, bytes_accessed=1, transcendentals=0)


def split(x):
    hi = x.astype(jnp.bfloat16)
    return hi, (x - hi.astype(jnp.float32)).astype(jnp.bfloat16)


def dot3(a_hi, a_lo, b_hi, b_lo):
    dot = functools.partial(jnp.dot, preferred_element_type=jnp.float32)
    return dot(a_hi, b_hi) + (dot(a_hi, b_lo) + dot(a_lo, b_hi))


def scale_kernel(place, *refs):
    parts, cores, (hi, lo) = refs[:4], refs[4], refs[-2:]
    group = jnp.concatenate([part[...] for part in parts], axis=0)
    scaled = dot3(*split(cores[0]), *split(group))
    hi[...], lo[...] = split(scaled.T)


def scale_into(place, parts, cores, line, previous, depth):
    width = parts[0][0].shape[1]
    rows = cores.shape[1]
    half = rows // 4
    tile = min(width, 1024)
    block = pl.BlockSpec((tile, rows), lambda i, place: (i, place[0]))
    shape = jax.ShapeDtypeStruct((width, depth), jnp.bfloat16)
    held = [] if previous is None else list(previous)
    return pl.pallas_call(
        scale_kernel,
        grid_spec=pltpu.PrefetchScalarGridSpec(
            num_scalar_prefetch=1,
            grid=(width // tile,),
            in_specs=[
                pl.BlockSpec((half, tile), functools.partial(lambda at, i, place: (at, i), at))
                for _, at in parts
            ]
            + [pl.BlockSpec((1, rows, rows), lambda i, place: (line, 0, 0))]
            + [pl.BlockSpec(memory_space=pl.ANY)] * len(held),
            out_specs=[block, block],
        ),
        out_shape=[shape, shape],
        input_output_aliases={} if previous is None else {6: 0, 7: 1},
        compiler_params=pltpu.CompilerParams(vmem_limit_bytes=SCALE_VMEM),
        cost_estimate=EARLY,
    )(place, *(a for a, _ in parts), cores, *held)


def blocks_kernel(per_col, col, slots, *refs):
    near, far, (out, held) = refs[:-3], refs[-3], refs[-2:]
    lines = len(near)
    rank = held.shape[1]
    together = 2 * per_col
    for s in range(lines):
        held[s * together : s * together + per_col] = near[s][...]
        held[s * together + per_col : (s + 1) * together] = far[s * per_col : (s + 1) * per_col]
    out[...] = jnp.zeros_like(out)
    me = col[0]
    for s in range(lines):
        for t in range(together):
            owner = me ^ (2 * s + t // per_col)
            slot = slots[owner * per_col + t % per_col]
            block = held[((slot // per_col) ^ me) * per_col + slot % per_col]
            row = (t + (me % 2) * per_col) % together
            out[s, pl.ds(pl.multiple_of(row * rank, rank), rank), t * rank : (t + 1) * rank] = block


def diagonal_blocks(col, slots, near, far):
    per_col, rank, _ = near[0].shape
    lines = len(near)
    size = 2 * per_col * rank
    return pl.pallas_call(
        functools.partial(blocks_kernel, per_col),
        grid_spec=pltpu.PrefetchScalarGridSpec(
            num_scalar_prefetch=2,
            grid=(1,),
            in_specs=[pl.BlockSpec(x.shape, lambda i, col, slots: (0, 0, 0)) for x in (*near, far)],
            out_specs=pl.BlockSpec((lines, size, size), lambda i, col, slots: (0, 0, 0)),
            scratch_shapes=[pltpu.VMEM((2 * lines * per_col, rank, rank), jnp.float32)],
        ),
        out_shape=jax.ShapeDtypeStruct((lines, size, size), jnp.float32),
        compiler_params=pltpu.CompilerParams(vmem_limit_bytes=SCALE_VMEM),
        cost_estimate=EARLY,
    )(col, slots, *near, far)


def update_kernel(trailing, hi, lo, right, *refs):
    out, right_hi, right_lo = refs[-3:]

    @pl.when(pl.program_id(0) == 0)
    def _():
        right_hi[...], right_lo[...] = split(right[...])

    out[...] = trailing[...] - dot3(hi[...], lo[...], right_hi[...], right_lo[...])


def update_chunk(start, trailing, left, right, previous):
    height = trailing.shape[0]
    depth, wide = right.shape
    tile = min(height, 512)
    here = pl.BlockSpec((tile, wide), lambda i: (i, start // wide))
    side = pl.BlockSpec((tile, depth), lambda i: (i, 0))
    held = [] if previous is None else [previous]
    return pl.pallas_call(
        update_kernel,
        grid=(height // tile,),
        in_specs=[here, side, side, pl.BlockSpec((depth, wide), lambda i: (0, 0))]
        + [pl.BlockSpec(memory_space=pl.ANY)] * len(held),
        out_specs=here,
        out_shape=jax.ShapeDtypeStruct(trailing.shape, jnp.float32),
        scratch_shapes=[pltpu.VMEM((depth, wide), jnp.bfloat16)] * 2,
        input_output_aliases={} if previous is None else {4: 0},
        compiler_params=pltpu.CompilerParams(vmem_limit_bytes=UPDATE_VMEM),
        cost_estimate=EARLY,
    )(trailing, *left, right, *held)


def body(planes, columns, trailing, panel_factors, vectors_t, inverse_lower_factors, slot_of_panel):
    lines = columns // 2
    rows = panel_factors.shape[0]
    width = trailing.shape[1]
    depth = rows * columns
    halves = columns // planes
    col = lax.axis_index("col")
    line = col // 2

    def across(x, bits):
        return lax.ppermute(x, "col", [(i, i ^ bits) for i in range(columns)])

    def along(x, moves):
        return lax.ppermute(x, "row", moves)

    eighth = width // 8

    def column_chunk(first, count):
        parts = []
        for h in range(halves):
            at = h * width + first * eighth
            parts.append(panel_factors[:, at : at + count * eighth])
        return jnp.stack(parts)

    after = lax.optimization_barrier

    everywhere = [lax.all_gather(column_chunk(*c), "row", axis=0, tiled=True) for c in CHUNKS]
    solved = lax.dot_general(
        vectors_t, inverse_lower_factors, (((2,), (2,)), ((0,), (0,))), precision=HIGHEST
    )
    cores = jnp.einsum("fdv,fpv->fdp", solved, solved, precision=HIGHEST)
    bit = 1
    while bit < planes:
        cores = cores + along(cores, [(i, i ^ bit) for i in range(planes)])
        bit *= 2
    bulk, cores = after((panel_factors, cores))
    near = [cores] + [across(cores, 2 * s) for s in range(1, lines)]

    cut = rows // 2
    gathered = [[[bulk], None]] + [[None, None] for _ in range(lines - 1)]
    single = [1 << i for i in range(lines.bit_length() - 1)]
    for s in single:
        gathered[s][0] = [across(bulk, 2 * s)]

    far = across(jnp.concatenate(near), 1)
    gathered[0][1] = [across(bulk, 1)]

    arrived, far, gathered[0][1] = after(([gathered[s][0] for s in single], far, gathered[0][1]))
    for s, x in zip(single, arrived):
        gathered[s][0] = x
    several = sorted((s for s in range(1, lines) if s not in single), key=lambda s: bin(s).count("1"))
    for s in several:
        low, high = s & -s, 1 << (s.bit_length() - 1)
        upper, lower = gathered[s ^ high][0], gathered[s ^ low][0]
        gathered[s][0] = [
            across(upper[0][:cut], 2 * high),
            across(lower[-1][-cut:], 2 * low),
        ]
    for s in single:
        gathered[s][1] = [across(x, 1) for x in gathered[s][0]]

    arrived, swapped, everywhere[0] = after(
        ([gathered[s][0] for s in several], [gathered[s][1] for s in single], everywhere[0])
    )
    for s, x in zip(several, arrived):
        gathered[s][0] = x
        gathered[s][1] = [across(part, 1) for part in x]
    for s, x in zip(single, swapped):
        gathered[s][1] = x

    def exchange(number):
        chunk = lax.all_to_all(everywhere[number], "col", split_axis=0, concat_axis=0, tiled=True)
        return chunk.reshape(depth, -1)

    chunks = [exchange(0)]
    blocks = diagonal_blocks(col.astype(jnp.int32).reshape(1), slot_of_panel, near, far)

    left = None
    for s in range(lines):
        place = (line ^ s).astype(jnp.int32).reshape(1)
        parts = []
        for group in gathered[s]:
            parts += [(group[0], 0), (group[0], 1)] if len(group) == 1 else [(x, 0) for x in group]
        left = scale_into(place, parts, blocks, s, left, depth)

    updated = None
    for number, (first, _) in enumerate(CHUNKS):
        if number + 1 < len(CHUNKS):
            if updated is None:
                everywhere[number + 1], left = after((everywhere[number + 1], left))
            else:
                everywhere[number + 1], updated = after((everywhere[number + 1], updated))
            chunks.append(exchange(number + 1))
        updated = update_chunk(first * eighth, trailing, left, chunks[number], updated)
    return updated


def solution(mesh):
    planes, columns = mesh.shape["row"], mesh.shape["col"]
    if columns != 2 * planes or planes & (planes - 1):
        raise ValueError("unsupported mesh")
    return jax.shard_map(
        functools.partial(body, planes, columns),
        mesh=mesh,
        in_specs=(
            P("row", "col"),
            P("col", "row"),
            P("col", None, None),
            P("col", "row", None),
            P(),
        ),
        out_specs=P("row", "col"),
        check_vma=False,
    )
```

```python
import functools

import jax
import jax.numpy as jnp
from jax import lax
from jax.experimental import pallas as pl
from jax.experimental.pallas import tpu as pltpu
from jax.sharding import PartitionSpec as P

GATHERS = ((0, 4), (4, 2), (6, 2))
CHUNKS = ((0, 0, 2), (0, 2, 2), (1, 4, 2), (2, 6, 2))
HIGHEST = lax.Precision.HIGHEST
SCALE_VMEM = 48 * 1024 * 1024
UPDATE_VMEM = 48 * 1024 * 1024
EARLY = pl.CostEstimate(flops=1, bytes_accessed=1, transcendentals=0)


def split(x):
    hi = x.astype(jnp.bfloat16)
    return hi, (x - hi.astype(jnp.float32)).astype(jnp.bfloat16)


def dot3(a_hi, a_lo, b_hi, b_lo):
    dot = functools.partial(jnp.dot, preferred_element_type=jnp.float32)
    return dot(a_hi, b_hi) + (dot(a_hi, b_lo) + dot(a_lo, b_hi))


def scale_kernel(place, *refs):
    parts, cores, (hi, lo) = refs[:4], refs[4], refs[-2:]
    group = jnp.concatenate([part[...] for part in parts], axis=0)
    scaled = dot3(*split(cores[0]), *split(group))
    hi[...], lo[...] = split(scaled.T)


def scale_into(place, parts, cores, line, previous, depth):
    width = parts[0][0].shape[1]
    rows = cores.shape[1]
    half = rows // 4
    tile = min(width, 1024)
    block = pl.BlockSpec((tile, rows), lambda i, place: (i, place[0]))
    shape = jax.ShapeDtypeStruct((width, depth), jnp.bfloat16)
    held = [] if previous is None else list(previous)
    return pl.pallas_call(
        scale_kernel,
        grid_spec=pltpu.PrefetchScalarGridSpec(
            num_scalar_prefetch=1,
            grid=(width // tile,),
            in_specs=[
                pl.BlockSpec((half, tile), functools.partial(lambda at, i, place: (at, i), at))
                for _, at in parts
            ]
            + [pl.BlockSpec((1, rows, rows), lambda i, place: (line, 0, 0))]
            + [pl.BlockSpec(memory_space=pl.ANY)] * len(held),
            out_specs=[block, block],
        ),
        out_shape=[shape, shape],
        input_output_aliases={} if previous is None else {6: 0, 7: 1},
        compiler_params=pltpu.CompilerParams(vmem_limit_bytes=SCALE_VMEM),
        cost_estimate=EARLY,
    )(place, *(a for a, _ in parts), cores, *held)


def blocks_kernel(per_col, col, slots, *refs):
    near, far, (out, held) = refs[:-3], refs[-3], refs[-2:]
    lines = len(near)
    rank = held.shape[1]
    together = 2 * per_col
    for s in range(lines):
        held[s * together : s * together + per_col] = near[s][...]
        held[s * together + per_col : (s + 1) * together] = far[s * per_col : (s + 1) * per_col]
    out[...] = jnp.zeros_like(out)
    me = col[0]
    for s in range(lines):
        for t in range(together):
            owner = me ^ (2 * s + t // per_col)
            slot = slots[owner * per_col + t % per_col]
            block = held[((slot // per_col) ^ me) * per_col + slot % per_col]
            row = (t + (me % 2) * per_col) % together
            out[s, pl.ds(pl.multiple_of(row * rank, rank), rank), t * rank : (t + 1) * rank] = block


def diagonal_blocks(col, slots, near, far):
    per_col, rank, _ = near[0].shape
    lines = len(near)
    size = 2 * per_col * rank
    return pl.pallas_call(
        functools.partial(blocks_kernel, per_col),
        grid_spec=pltpu.PrefetchScalarGridSpec(
            num_scalar_prefetch=2,
            grid=(1,),
            in_specs=[pl.BlockSpec(x.shape, lambda i, col, slots: (0, 0, 0)) for x in (*near, far)],
            out_specs=pl.BlockSpec((lines, size, size), lambda i, col, slots: (0, 0, 0)),
            scratch_shapes=[pltpu.VMEM((2 * lines * per_col, rank, rank), jnp.float32)],
        ),
        out_shape=jax.ShapeDtypeStruct((lines, size, size), jnp.float32),
        compiler_params=pltpu.CompilerParams(vmem_limit_bytes=SCALE_VMEM),
        cost_estimate=EARLY,
    )(col, slots, *near, far)


def update_kernel(trailing, hi, lo, right, *refs):
    out, right_hi, right_lo = refs[-3:]

    @pl.when(pl.program_id(0) == 0)
    def _():
        right_hi[...], right_lo[...] = split(right[...])

    out[...] = trailing[...] - dot3(hi[...], lo[...], right_hi[...], right_lo[...])


def update_chunk(start, trailing, left, right, previous):
    height = trailing.shape[0]
    depth, wide = right.shape
    tile = min(height, 1024)
    here = pl.BlockSpec((tile, wide), lambda i: (i, start // wide))
    side = pl.BlockSpec((tile, depth), lambda i: (i, 0))
    held = [] if previous is None else [previous]
    return pl.pallas_call(
        update_kernel,
        grid=(height // tile,),
        in_specs=[here, side, side, pl.BlockSpec((depth, wide), lambda i: (0, 0))]
        + [pl.BlockSpec(memory_space=pl.ANY)] * len(held),
        out_specs=here,
        out_shape=jax.ShapeDtypeStruct(trailing.shape, jnp.float32),
        scratch_shapes=[pltpu.VMEM((depth, wide), jnp.bfloat16)] * 2,
        input_output_aliases={} if previous is None else {4: 0},
        compiler_params=pltpu.CompilerParams(vmem_limit_bytes=UPDATE_VMEM),
        cost_estimate=EARLY,
    )(trailing, *left, right, *held)


def body(planes, columns, trailing, panel_factors, vectors_t, inverse_lower_factors, slot_of_panel):
    lines = columns // 2
    rows = panel_factors.shape[0]
    width = trailing.shape[1]
    depth = rows * columns
    halves = columns // planes
    col = lax.axis_index("col")
    line = col // 2

    def across(x, bits):
        return lax.ppermute(x, "col", [(i, i ^ bits) for i in range(columns)])

    def along(x, moves):
        return lax.ppermute(x, "row", moves)

    eighth = width // 8

    def column_chunk(first, count):
        parts = []
        for h in range(halves):
            at = h * width + first * eighth
            parts.append(panel_factors[:, at : at + count * eighth])
        return jnp.stack(parts)

    after = lax.optimization_barrier

    everywhere = [lax.all_gather(column_chunk(*g), "row", axis=0, tiled=True) for g in GATHERS]
    cut = rows // 2
    own = [panel_factors[:cut], panel_factors[cut:]]
    gathered = [[own, None]] + [[None, None] for _ in range(lines - 1)]
    single = [1 << i for i in range(lines.bit_length() - 1)]
    for s in single:
        gathered[s][0] = [across(x, 2 * s) for x in own]
    solved = lax.dot_general(
        vectors_t, inverse_lower_factors, (((2,), (2,)), ((0,), (0,))), precision=HIGHEST
    )
    cores = jnp.einsum("fdv,fpv->fdp", solved, solved, precision=HIGHEST)
    bit = 1
    while bit < planes:
        cores = cores + along(cores, [(i, i ^ bit) for i in range(planes)])
        bit *= 2

    arrived, cores = after(([gathered[s][0] for s in single], cores))
    for s, x in zip(single, arrived):
        gathered[s][0] = x
    near = [cores] + [across(cores, 2 * s) for s in range(1, lines)]
    several = sorted((s for s in range(1, lines) if s not in single), key=lambda s: bin(s).count("1"))
    for s in several:
        low, high = s & -s, 1 << (s.bit_length() - 1)
        gathered[s][0] = [
            across(gathered[s ^ high][0][0], 2 * high),
            across(gathered[s ^ low][0][1], 2 * low),
        ]

    arrived, near, everywhere[0] = after(([gathered[s][0] for s in several], near, everywhere[0]))
    for s, x in zip(several, arrived):
        gathered[s][0] = x
    far = across(jnp.concatenate(near), 1)
    gathered[0] = [[panel_factors], [across(panel_factors, 1)]]
    for s in range(1, lines):
        gathered[s][1] = [across(x, 1) for x in gathered[s][0]]

    def exchange(number):
        source, first, count = CHUNKS[number]
        sent = everywhere[source]
        if GATHERS[source][1] != count:
            at = (first - GATHERS[source][0]) * eighth
            sent = sent[:, :, at : at + count * eighth]
        chunk = lax.all_to_all(sent, "col", split_axis=0, concat_axis=0, tiled=True)
        return chunk.reshape(depth, -1)

    chunks = [exchange(0)]
    blocks = diagonal_blocks(col.astype(jnp.int32).reshape(1), slot_of_panel, near, far)

    left = None
    for s in range(lines):
        place = (line ^ s).astype(jnp.int32).reshape(1)
        parts = []
        for group in gathered[s]:
            parts += [(group[0], 0), (group[0], 1)] if len(group) == 1 else [(x, 0) for x in group]
        left = scale_into(place, parts, blocks, s, left, depth)

    updated = None
    for number, (_, first, _) in enumerate(CHUNKS):
        if number + 1 < len(CHUNKS):
            source = CHUNKS[number + 1][0]
            if updated is None:
                everywhere[source], left = after((everywhere[source], left))
            else:
                everywhere[source], updated = after((everywhere[source], updated))
            chunks.append(exchange(number + 1))
        updated = update_chunk(first * eighth, trailing, left, chunks[number], updated)
    return updated


def solution(mesh):
    planes, columns = mesh.shape["row"], mesh.shape["col"]
    if columns != 2 * planes or planes & (planes - 1):
        raise ValueError("unsupported mesh")
    return jax.shard_map(
        functools.partial(body, planes, columns),
        mesh=mesh,
        in_specs=(
            P("row", "col"),
            P("col", "row"),
            P("col", None, None),
            P("col", "row", None),
            P(),
        ),
        out_specs=P("row", "col"),
        check_vma=False,
    )
```

```python
import functools

import jax
import jax.numpy as jnp
from jax import lax
from jax.experimental import pallas as pl
from jax.experimental.pallas import tpu as pltpu
from jax.sharding import PartitionSpec as P

GATHERS = ((0, 3), (3, 3), (6, 2))
CHUNKS = ((0, 0, 3), (1, 3, 3), (2, 6, 2))
HIGHEST = lax.Precision.HIGHEST
SCALE_VMEM = 48 * 1024 * 1024
UPDATE_VMEM = 48 * 1024 * 1024
EARLY = pl.CostEstimate(flops=1, bytes_accessed=1, transcendentals=0)


def split(x):
    hi = x.astype(jnp.bfloat16)
    return hi, (x - hi.astype(jnp.float32)).astype(jnp.bfloat16)


def dot3(a_hi, a_lo, b_hi, b_lo):
    dot = functools.partial(jnp.dot, preferred_element_type=jnp.float32)
    return dot(a_hi, b_hi) + (dot(a_hi, b_lo) + dot(a_lo, b_hi))


def scale_kernel(place, *refs):
    parts, cores, (hi, lo) = refs[:4], refs[4], refs[-2:]
    group = jnp.concatenate([part[...] for part in parts], axis=0)
    scaled = dot3(*split(cores[0]), *split(group))
    hi[...], lo[...] = split(scaled.T)


def scale_into(place, parts, cores, line, previous, depth):
    width = parts[0][0].shape[1]
    rows = cores.shape[1]
    half = rows // 4
    tile = min(width, 1024)
    block = pl.BlockSpec((tile, rows), lambda i, place: (i, place[0]))
    shape = jax.ShapeDtypeStruct((width, depth), jnp.bfloat16)
    held = [] if previous is None else list(previous)
    return pl.pallas_call(
        scale_kernel,
        grid_spec=pltpu.PrefetchScalarGridSpec(
            num_scalar_prefetch=1,
            grid=(width // tile,),
            in_specs=[
                pl.BlockSpec((half, tile), functools.partial(lambda at, i, place: (at, i), at))
                for _, at in parts
            ]
            + [pl.BlockSpec((1, rows, rows), lambda i, place: (line, 0, 0))]
            + [pl.BlockSpec(memory_space=pl.ANY)] * len(held),
            out_specs=[block, block],
        ),
        out_shape=[shape, shape],
        input_output_aliases={} if previous is None else {6: 0, 7: 1},
        compiler_params=pltpu.CompilerParams(vmem_limit_bytes=SCALE_VMEM),
        cost_estimate=EARLY,
    )(place, *(a for a, _ in parts), cores, *held)


def blocks_kernel(per_col, col, slots, *refs):
    near, far, (out, held) = refs[:-3], refs[-3], refs[-2:]
    lines = len(near)
    rank = held.shape[1]
    together = 2 * per_col
    for s in range(lines):
        held[s * together : s * together + per_col] = near[s][...]
        held[s * together + per_col : (s + 1) * together] = far[s * per_col : (s + 1) * per_col]
    out[...] = jnp.zeros_like(out)
    me = col[0]
    for s in range(lines):
        for t in range(together):
            owner = me ^ (2 * s + t // per_col)
            slot = slots[owner * per_col + t % per_col]
            block = held[((slot // per_col) ^ me) * per_col + slot % per_col]
            row = (t + (me % 2) * per_col) % together
            out[s, pl.ds(pl.multiple_of(row * rank, rank), rank), t * rank : (t + 1) * rank] = block


def diagonal_blocks(col, slots, near, far):
    per_col, rank, _ = near[0].shape
    lines = len(near)
    size = 2 * per_col * rank
    return pl.pallas_call(
        functools.partial(blocks_kernel, per_col),
        grid_spec=pltpu.PrefetchScalarGridSpec(
            num_scalar_prefetch=2,
            grid=(1,),
            in_specs=[pl.BlockSpec(x.shape, lambda i, col, slots: (0, 0, 0)) for x in (*near, far)],
            out_specs=pl.BlockSpec((lines, size, size), lambda i, col, slots: (0, 0, 0)),
            scratch_shapes=[pltpu.VMEM((2 * lines * per_col, rank, rank), jnp.float32)],
        ),
        out_shape=jax.ShapeDtypeStruct((lines, size, size), jnp.float32),
        compiler_params=pltpu.CompilerParams(vmem_limit_bytes=SCALE_VMEM),
        cost_estimate=EARLY,
    )(col, slots, *near, far)


def update_kernel(trailing, hi, lo, right, *refs):
    out, right_hi, right_lo = refs[-3:]

    @pl.when(pl.program_id(0) == 0)
    def _():
        right_hi[...], right_lo[...] = split(right[...])

    out[...] = trailing[...] - dot3(hi[...], lo[...], right_hi[...], right_lo[...])


def update_chunk(start, trailing, left, right, previous):
    height = trailing.shape[0]
    depth, wide = right.shape
    tile = min(height, 1024)
    here = pl.BlockSpec((tile, wide), lambda i: (i, start // wide))
    side = pl.BlockSpec((tile, depth), lambda i: (i, 0))
    held = [] if previous is None else [previous]
    return pl.pallas_call(
        update_kernel,
        grid=(height // tile,),
        in_specs=[here, side, side, pl.BlockSpec((depth, wide), lambda i: (0, 0))]
        + [pl.BlockSpec(memory_space=pl.ANY)] * len(held),
        out_specs=here,
        out_shape=jax.ShapeDtypeStruct(trailing.shape, jnp.float32),
        scratch_shapes=[pltpu.VMEM((depth, wide), jnp.bfloat16)] * 2,
        input_output_aliases={} if previous is None else {4: 0},
        compiler_params=pltpu.CompilerParams(vmem_limit_bytes=UPDATE_VMEM),
        cost_estimate=EARLY,
    )(trailing, *left, right, *held)


def body(planes, columns, trailing, panel_factors, vectors_t, inverse_lower_factors, slot_of_panel):
    lines = columns // 2
    rows = panel_factors.shape[0]
    width = trailing.shape[1]
    depth = rows * columns
    halves = columns // planes
    col = lax.axis_index("col")
    line = col // 2

    def across(x, bits):
        return lax.ppermute(x, "col", [(i, i ^ bits) for i in range(columns)])

    def along(x, moves):
        return lax.ppermute(x, "row", moves)

    eighth = width // 8

    def column_chunk(first, count):
        parts = []
        for h in range(halves):
            at = h * width + first * eighth
            parts.append(panel_factors[:, at : at + count * eighth])
        return jnp.stack(parts)

    after = lax.optimization_barrier

    everywhere = [lax.all_gather(column_chunk(*g), "row", axis=0, tiled=True) for g in GATHERS]
    cut = rows // 2
    own = [panel_factors[:cut], panel_factors[cut:]]
    gathered = [[own, None]] + [[None, None] for _ in range(lines - 1)]
    single = [1 << i for i in range(lines.bit_length() - 1)]
    for s in single:
        gathered[s][0] = [across(x, 2 * s) for x in own]
    solved = lax.dot_general(
        vectors_t, inverse_lower_factors, (((2,), (2,)), ((0,), (0,))), precision=HIGHEST
    )
    cores = jnp.einsum("fdv,fpv->fdp", solved, solved, precision=HIGHEST)
    bit = 1
    while bit < planes:
        cores = cores + along(cores, [(i, i ^ bit) for i in range(planes)])
        bit *= 2

    near = [cores] + [across(cores, 2 * s) for s in range(1, lines)]

    arrived, near = after(([gathered[s][0] for s in single], near))
    for s, x in zip(single, arrived):
        gathered[s][0] = x
    several = sorted((s for s in range(1, lines) if s not in single), key=lambda s: bin(s).count("1"))
    for s in several:
        low, high = s & -s, 1 << (s.bit_length() - 1)
        gathered[s][0] = [
            across(gathered[s ^ high][0][0], 2 * high),
            across(gathered[s ^ low][0][1], 2 * low),
        ]
    far = across(jnp.concatenate(near), 1)
    blocks = diagonal_blocks(col.astype(jnp.int32).reshape(1), slot_of_panel, near, far)

    def scale(s, left):
        place = (line ^ s).astype(jnp.int32).reshape(1)
        groups = gathered[s][0], [across(x, 1) for x in gathered[s][0]]
        parts = [(x, 0) for group in groups for x in group]
        if s == 0:
            whole = [panel_factors, across(panel_factors, 1)]
            parts = [(x, half) for x in whole for half in range(2)]
        return scale_into(place, parts, blocks, s, left, depth)

    left = None
    for s in [0] + single:
        left = scale(s, left)

    def exchange(number):
        source, first, count = CHUNKS[number]
        sent = everywhere[source]
        if GATHERS[source][1] != count:
            at = (first - GATHERS[source][0]) * eighth
            sent = sent[:, :, at : at + count * eighth]
        chunk = lax.all_to_all(sent, "col", split_axis=0, concat_axis=0, tiled=True)
        return chunk.reshape(depth, -1)

    arrived, left, everywhere[0] = after(([gathered[s][0] for s in several], left, everywhere[0]))
    chunks = [exchange(0)]
    for s, x in zip(several, arrived):
        gathered[s][0] = x
    for s in several:
        left = scale(s, left)

    updated = None
    for number, (_, first, _) in enumerate(CHUNKS):
        if number + 1 < len(CHUNKS):
            source = CHUNKS[number + 1][0]
            if updated is None:
                everywhere[source], left = after((everywhere[source], left))
            else:
                everywhere[source], updated = after((everywhere[source], updated))
            chunks.append(exchange(number + 1))
        updated = update_chunk(first * eighth, trailing, left, chunks[number], updated)
    return updated


def solution(mesh):
    planes, columns = mesh.shape["row"], mesh.shape["col"]
    if columns != 2 * planes or planes & (planes - 1):
        raise ValueError("unsupported mesh")
    return jax.shard_map(
        functools.partial(body, planes, columns),
        mesh=mesh,
        in_specs=(
            P("row", "col"),
            P("col", "row"),
            P("col", None, None),
            P("col", "row", None),
            P(),
        ),
        out_specs=P("row", "col"),
        check_vma=False,
    )
```

```python
import functools

import jax
import jax.numpy as jnp
from jax import lax
from jax.experimental import pallas as pl
from jax.experimental.pallas import tpu as pltpu
from jax.sharding import PartitionSpec as P

GATHERS = ((0, 3), (4, 2), (6, 2))
HOPPED = (3, 1)
CHUNKS = ((0, 3), (3, 3), (6, 2))
HIGHEST = lax.Precision.HIGHEST
SCALE_VMEM = 48 * 1024 * 1024
UPDATE_VMEM = 48 * 1024 * 1024
EARLY = pl.CostEstimate(flops=1, bytes_accessed=1, transcendentals=0)


def split(x):
    hi = x.astype(jnp.bfloat16)
    return hi, (x - hi.astype(jnp.float32)).astype(jnp.bfloat16)


def dot3(a_hi, a_lo, b_hi, b_lo):
    dot = functools.partial(jnp.dot, preferred_element_type=jnp.float32)
    return dot(a_hi, b_hi) + (dot(a_hi, b_lo) + dot(a_lo, b_hi))


def scale_kernel(place, *refs):
    parts, cores, (hi, lo) = refs[:4], refs[4], refs[-2:]
    group = jnp.concatenate([part[...] for part in parts], axis=0)
    scaled = dot3(*split(cores[0]), *split(group))
    hi[...], lo[...] = split(scaled.T)


def scale_into(place, parts, cores, line, previous, depth):
    width = parts[0][0].shape[1]
    rows = cores.shape[1]
    half = rows // 4
    tile = min(width, 1024)
    block = pl.BlockSpec((tile, rows), lambda i, place: (i, place[0]))
    shape = jax.ShapeDtypeStruct((width, depth), jnp.bfloat16)
    held = [] if previous is None else list(previous)
    return pl.pallas_call(
        scale_kernel,
        grid_spec=pltpu.PrefetchScalarGridSpec(
            num_scalar_prefetch=1,
            grid=(width // tile,),
            in_specs=[
                pl.BlockSpec((half, tile), functools.partial(lambda at, i, place: (at, i), at))
                for _, at in parts
            ]
            + [pl.BlockSpec((1, rows, rows), lambda i, place: (line, 0, 0))]
            + [pl.BlockSpec(memory_space=pl.ANY)] * len(held),
            out_specs=[block, block],
        ),
        out_shape=[shape, shape],
        input_output_aliases={} if previous is None else {6: 0, 7: 1},
        compiler_params=pltpu.CompilerParams(vmem_limit_bytes=SCALE_VMEM),
        cost_estimate=EARLY,
    )(place, *(a for a, _ in parts), cores, *held)


def blocks_kernel(per_col, col, slots, *refs):
    near, far, (out, held) = refs[:-3], refs[-3], refs[-2:]
    lines = len(near)
    rank = held.shape[1]
    together = 2 * per_col
    for s in range(lines):
        held[s * together : s * together + per_col] = near[s][...]
        held[s * together + per_col : (s + 1) * together] = far[s * per_col : (s + 1) * per_col]
    out[...] = jnp.zeros_like(out)
    me = col[0]
    for s in range(lines):
        for t in range(together):
            owner = me ^ (2 * s + t // per_col)
            slot = slots[owner * per_col + t % per_col]
            block = held[((slot // per_col) ^ me) * per_col + slot % per_col]
            row = (t + (me % 2) * per_col) % together
            out[s, pl.ds(pl.multiple_of(row * rank, rank), rank), t * rank : (t + 1) * rank] = block


def diagonal_blocks(col, slots, near, far):
    per_col, rank, _ = near[0].shape
    lines = len(near)
    size = 2 * per_col * rank
    return pl.pallas_call(
        functools.partial(blocks_kernel, per_col),
        grid_spec=pltpu.PrefetchScalarGridSpec(
            num_scalar_prefetch=2,
            grid=(1,),
            in_specs=[pl.BlockSpec(x.shape, lambda i, col, slots: (0, 0, 0)) for x in (*near, far)],
            out_specs=pl.BlockSpec((lines, size, size), lambda i, col, slots: (0, 0, 0)),
            scratch_shapes=[pltpu.VMEM((2 * lines * per_col, rank, rank), jnp.float32)],
        ),
        out_shape=jax.ShapeDtypeStruct((lines, size, size), jnp.float32),
        compiler_params=pltpu.CompilerParams(vmem_limit_bytes=SCALE_VMEM),
        cost_estimate=EARLY,
    )(col, slots, *near, far)


def lay_kernel(planes, plane, *refs):
    sources, rest, (out, sems) = refs[: 2 * planes - 1], refs[-3], refs[-2:]
    blocks = out.shape[0] // planes
    wide = sources[0].shape[2]
    tail = pltpu.make_async_copy(rest, out.at[:, :, pl.ds(wide, rest.shape[2])], sems.at[planes])
    tail.start()
    for z in range(planes):

        @pl.when(plane[0] == z)
        def _():
            copies = [
                pltpu.make_async_copy(
                    sources[planes - 1 + q - z],
                    out.at[pl.ds(q * blocks, blocks), :, pl.ds(0, wide)],
                    sems.at[q],
                )
                for q in range(planes)
            ]
            for copy in copies:
                copy.start()
            for copy in copies:
                copy.wait()

    tail.wait()


def lay(plane, sources, rest):
    planes = (len(sources) + 1) // 2
    shape = sources[0].shape
    result = (rest.shape[0], shape[1], shape[2] + rest.shape[2])
    return pl.pallas_call(
        functools.partial(lay_kernel, planes),
        grid_spec=pltpu.PrefetchScalarGridSpec(
            num_scalar_prefetch=1,
            grid=(1,),
            in_specs=[pl.BlockSpec(memory_space=pl.ANY)] * (len(sources) + 1),
            out_specs=pl.BlockSpec(result, lambda i, plane: (0, 0, 0)),
            scratch_shapes=[pltpu.SemaphoreType.DMA((planes + 1,))],
        ),
        out_shape=jax.ShapeDtypeStruct(result, jnp.float32),
        compiler_params=pltpu.CompilerParams(vmem_limit_bytes=SCALE_VMEM),
        cost_estimate=EARLY,
    )(plane, *sources, rest)


def update_kernel(trailing, hi, lo, right, *refs):
    out, right_hi, right_lo = refs[-3:]

    @pl.when(pl.program_id(0) == 0)
    def _():
        right_hi[...], right_lo[...] = split(right[...])

    out[...] = trailing[...] - dot3(hi[...], lo[...], right_hi[...], right_lo[...])


def update_chunk(start, trailing, left, right, previous):
    height = trailing.shape[0]
    depth, wide = right.shape
    tile = min(height, 1024)
    here = pl.BlockSpec((tile, wide), lambda i: (i, start // wide))
    side = pl.BlockSpec((tile, depth), lambda i: (i, 0))
    held = [] if previous is None else [previous]
    return pl.pallas_call(
        update_kernel,
        grid=(height // tile,),
        in_specs=[here, side, side, pl.BlockSpec((depth, wide), lambda i: (0, 0))]
        + [pl.BlockSpec(memory_space=pl.ANY)] * len(held),
        out_specs=here,
        out_shape=jax.ShapeDtypeStruct(trailing.shape, jnp.float32),
        scratch_shapes=[pltpu.VMEM((depth, wide), jnp.bfloat16)] * 2,
        input_output_aliases={} if previous is None else {4: 0},
        compiler_params=pltpu.CompilerParams(vmem_limit_bytes=UPDATE_VMEM),
        cost_estimate=EARLY,
    )(trailing, *left, right, *held)


def body(planes, columns, trailing, panel_factors, vectors_t, inverse_lower_factors, slot_of_panel):
    lines = columns // 2
    rows = panel_factors.shape[0]
    width = trailing.shape[1]
    depth = rows * columns
    halves = columns // planes
    col = lax.axis_index("col")
    line = col // 2

    def across(x, bits):
        return lax.ppermute(x, "col", [(i, i ^ bits) for i in range(columns)])

    def along(x, moves):
        return lax.ppermute(x, "row", moves)

    eighth = width // 8

    def column_chunk(first, count):
        parts = []
        for h in range(halves):
            at = h * width + first * eighth
            parts.append(panel_factors[:, at : at + count * eighth])
        return jnp.stack(parts)

    after = lax.optimization_barrier

    everywhere = [lax.all_gather(column_chunk(*g), "row", axis=0, tiled=True) for g in GATHERS]
    cut = rows // 2
    own = [panel_factors[:cut], panel_factors[cut:]]
    gathered = [[own, None]] + [[[None, None], None] for _ in range(lines - 1)]
    single = [1 << i for i in range(lines.bit_length() - 1)]

    def early(s):
        return 0 if s == 1 else 1

    for s in single:
        gathered[s][0][early(s)] = across(own[early(s)], 2 * s)
    solved = lax.dot_general(
        vectors_t, inverse_lower_factors, (((2,), (2,)), ((0,), (0,))), precision=HIGHEST
    )
    cores = jnp.einsum("fdv,fpv->fdp", solved, solved, precision=HIGHEST)
    bit = 1
    while bit < planes:
        cores = cores + along(cores, [(i, i ^ bit) for i in range(planes)])
        bit *= 2

    arrived, cores, bulk = after(([gathered[s][0][early(s)] for s in single], cores, own))
    near = [cores] + [across(cores, 2 * s) for s in range(1, lines)]
    for s, x in zip(single, arrived):
        gathered[s][0][early(s)] = x
        gathered[s][0][1 - early(s)] = across(bulk[1 - early(s)], 2 * s)

    mine = column_chunk(*HOPPED)
    arrived, near, mine = after(([gathered[s][0] for s in single], near, mine))
    for s, x in zip(single, arrived):
        gathered[s][0] = x
    several = sorted((s for s in range(1, lines) if s not in single), key=lambda s: bin(s).count("1"))
    for s in several:
        low, high = s & -s, 1 << (s.bit_length() - 1)
        gathered[s][0] = [
            across(gathered[s ^ high][0][0], 2 * high),
            across(gathered[s ^ low][0][1], 2 * low),
        ]

    from_above, from_below = [mine], [mine]

    def hop(d):
        from_above.append(along(from_above[-1], [(p, p - 1) for p in range(1, planes - d + 1)]))
        from_below.append(along(from_below[-1], [(p, p + 1) for p in range(d - 1, planes - 1)]))

    hop(1)
    far = across(jnp.concatenate(near), 1)
    blocks = diagonal_blocks(col.astype(jnp.int32).reshape(1), slot_of_panel, near, far)

    def scale(s, left):
        place = (line ^ s).astype(jnp.int32).reshape(1)
        groups = gathered[s][0], [across(x, 1) for x in gathered[s][0]]
        parts = [(x, 0) for group in groups for x in group]
        if s == 0:
            whole = [panel_factors, across(panel_factors, 1)]
            parts = [(x, half) for x in whole for half in range(2)]
        return scale_into(place, parts, blocks, s, left, depth)

    left = None
    for s in [0] + single:
        left = scale(s, left)

    def exchange(number):
        chunk = lax.all_to_all(everywhere[number], "col", split_axis=0, concat_axis=0, tiled=True)
        return chunk.reshape(depth, -1)

    arrived, left, everywhere[0], hopped = after(
        ([gathered[s][0] for s in several], left, everywhere[0], (from_above[-1], from_below[-1]))
    )
    from_above[-1], from_below[-1] = hopped
    chunks = [exchange(0)]
    for s, x in zip(several, arrived):
        gathered[s][0] = x
    for d in range(2, planes):
        hop(d)
    for s in several:
        left = scale(s, left)
    plane = lax.axis_index("row").astype(jnp.int32).reshape(1)
    everywhere[1] = lay(plane, from_below[:0:-1] + [mine] + from_above[1:], everywhere[1])

    updated = None
    for number, (first, _) in enumerate(CHUNKS):
        later = number + 1
        if later < len(CHUNKS):
            if updated is None:
                everywhere[later], left = after((everywhere[later], left))
            else:
                everywhere[later], updated = after((everywhere[later], updated))
            chunks.append(exchange(later))
        updated = update_chunk(first * eighth, trailing, left, chunks[number], updated)
    return updated


def solution(mesh):
    planes, columns = mesh.shape["row"], mesh.shape["col"]
    if columns != 2 * planes or planes & (planes - 1):
        raise ValueError("unsupported mesh")
    return jax.shard_map(
        functools.partial(body, planes, columns),
        mesh=mesh,
        in_specs=(
            P("row", "col"),
            P("col", "row"),
            P("col", None, None),
            P("col", "row", None),
            P(),
        ),
        out_specs=P("row", "col"),
        check_vma=False,
    )
```

```python
import functools

import jax
import jax.numpy as jnp
from jax import lax
from jax.experimental import pallas as pl
from jax.experimental.pallas import tpu as pltpu
from jax.sharding import PartitionSpec as P

GATHERS = ((0, 3), (4, 2), (6, 2))
HOPPED = (3, 1)
CHUNKS = ((0, 3), (3, 3), (6, 2))
HIGHEST = lax.Precision.HIGHEST
SCALE_VMEM = 48 * 1024 * 1024
UPDATE_VMEM = 48 * 1024 * 1024
EARLY = pl.CostEstimate(flops=1, bytes_accessed=1, transcendentals=0)


def split(x):
    hi = x.astype(jnp.bfloat16)
    return hi, (x - hi.astype(jnp.float32)).astype(jnp.bfloat16)


def dot3(a_hi, a_lo, b_hi, b_lo):
    dot = functools.partial(jnp.dot, preferred_element_type=jnp.float32)
    return dot(a_hi, b_hi) + (dot(a_hi, b_lo) + dot(a_lo, b_hi))


def scale_kernel(place, *refs):
    parts, cores, (hi, lo) = refs[:4], refs[4], refs[-2:]
    group = jnp.concatenate([part[...] for part in parts], axis=0)
    scaled = dot3(*split(cores[0]), *split(group))
    hi[...], lo[...] = split(scaled.T)


def scale_into(place, parts, cores, line, previous, depth):
    width = parts[0][0].shape[1]
    rows = cores.shape[1]
    half = rows // 4
    tile = min(width, 1024)
    block = pl.BlockSpec((tile, rows), lambda i, place: (i, place[0]))
    shape = jax.ShapeDtypeStruct((width, depth), jnp.bfloat16)
    held = [] if previous is None else list(previous)
    return pl.pallas_call(
        scale_kernel,
        grid_spec=pltpu.PrefetchScalarGridSpec(
            num_scalar_prefetch=1,
            grid=(width // tile,),
            in_specs=[
                pl.BlockSpec((half, tile), functools.partial(lambda at, i, place: (at, i), at))
                for _, at in parts
            ]
            + [pl.BlockSpec((1, rows, rows), lambda i, place: (line, 0, 0))]
            + [pl.BlockSpec(memory_space=pl.ANY)] * len(held),
            out_specs=[block, block],
        ),
        out_shape=[shape, shape],
        input_output_aliases={} if previous is None else {6: 0, 7: 1},
        compiler_params=pltpu.CompilerParams(vmem_limit_bytes=SCALE_VMEM),
        cost_estimate=EARLY,
    )(place, *(a for a, _ in parts), cores, *held)


def blocks_kernel(per_col, col, slots, *refs):
    near, far, (out, held) = refs[:-3], refs[-3], refs[-2:]
    lines = len(near)
    rank = held.shape[1]
    together = 2 * per_col
    for s in range(lines):
        held[s * together : s * together + per_col] = near[s][...]
        held[s * together + per_col : (s + 1) * together] = far[s * per_col : (s + 1) * per_col]
    out[...] = jnp.zeros_like(out)
    me = col[0]
    for s in range(lines):
        for t in range(together):
            owner = me ^ (2 * s + t // per_col)
            slot = slots[owner * per_col + t % per_col]
            block = held[((slot // per_col) ^ me) * per_col + slot % per_col]
            row = (t + (me % 2) * per_col) % together
            out[s, pl.ds(pl.multiple_of(row * rank, rank), rank), t * rank : (t + 1) * rank] = block


def diagonal_blocks(col, slots, near, far):
    per_col, rank, _ = near[0].shape
    lines = len(near)
    size = 2 * per_col * rank
    return pl.pallas_call(
        functools.partial(blocks_kernel, per_col),
        grid_spec=pltpu.PrefetchScalarGridSpec(
            num_scalar_prefetch=2,
            grid=(1,),
            in_specs=[pl.BlockSpec(x.shape, lambda i, col, slots: (0, 0, 0)) for x in (*near, far)],
            out_specs=pl.BlockSpec((lines, size, size), lambda i, col, slots: (0, 0, 0)),
            scratch_shapes=[pltpu.VMEM((2 * lines * per_col, rank, rank), jnp.float32)],
        ),
        out_shape=jax.ShapeDtypeStruct((lines, size, size), jnp.float32),
        compiler_params=pltpu.CompilerParams(vmem_limit_bytes=SCALE_VMEM),
        cost_estimate=EARLY,
    )(col, slots, *near, far)


def lay_kernel(planes, plane, *refs):
    sources, rest, (out, sems) = refs[: 2 * planes - 1], refs[-3], refs[-2:]
    blocks = out.shape[0] // planes
    wide = sources[0].shape[2]
    tail = pltpu.make_async_copy(rest, out.at[:, :, pl.ds(wide, rest.shape[2])], sems.at[planes])
    tail.start()
    for z in range(planes):

        @pl.when(plane[0] == z)
        def _():
            copies = [
                pltpu.make_async_copy(
                    sources[planes - 1 + q - z],
                    out.at[pl.ds(q * blocks, blocks), :, pl.ds(0, wide)],
                    sems.at[q],
                )
                for q in range(planes)
            ]
            for copy in copies:
                copy.start()
            for copy in copies:
                copy.wait()

    tail.wait()


def lay(plane, sources, rest):
    planes = (len(sources) + 1) // 2
    shape = sources[0].shape
    result = (rest.shape[0], shape[1], shape[2] + rest.shape[2])
    return pl.pallas_call(
        functools.partial(lay_kernel, planes),
        grid_spec=pltpu.PrefetchScalarGridSpec(
            num_scalar_prefetch=1,
            grid=(1,),
            in_specs=[pl.BlockSpec(memory_space=pl.ANY)] * (len(sources) + 1),
            out_specs=pl.BlockSpec(result, lambda i, plane: (0, 0, 0)),
            scratch_shapes=[pltpu.SemaphoreType.DMA((planes + 1,))],
        ),
        out_shape=jax.ShapeDtypeStruct(result, jnp.float32),
        compiler_params=pltpu.CompilerParams(vmem_limit_bytes=SCALE_VMEM),
        cost_estimate=EARLY,
    )(plane, *sources, rest)


def update_kernel(trailing, hi, lo, right, *refs):
    out, right_hi, right_lo = refs[-3:]

    @pl.when(pl.program_id(0) == 0)
    def _():
        right_hi[...], right_lo[...] = split(right[...])

    out[...] = trailing[...] - dot3(hi[...], lo[...], right_hi[...], right_lo[...])


def update_chunk(start, trailing, left, right, previous):
    height = trailing.shape[0]
    depth, wide = right.shape
    tile = min(height, 1024)
    here = pl.BlockSpec((tile, wide), lambda i: (i, start // wide))
    side = pl.BlockSpec((tile, depth), lambda i: (i, 0))
    held = [] if previous is None else [previous]
    return pl.pallas_call(
        update_kernel,
        grid=(height // tile,),
        in_specs=[here, side, side, pl.BlockSpec((depth, wide), lambda i: (0, 0))]
        + [pl.BlockSpec(memory_space=pl.ANY)] * len(held),
        out_specs=here,
        out_shape=jax.ShapeDtypeStruct(trailing.shape, jnp.float32),
        scratch_shapes=[pltpu.VMEM((depth, wide), jnp.bfloat16)] * 2,
        input_output_aliases={} if previous is None else {4: 0},
        compiler_params=pltpu.CompilerParams(vmem_limit_bytes=UPDATE_VMEM),
        cost_estimate=EARLY,
    )(trailing, *left, right, *held)


def body(planes, columns, trailing, panel_factors, vectors_t, inverse_lower_factors, slot_of_panel):
    lines = columns // 2
    rows = panel_factors.shape[0]
    width = trailing.shape[1]
    depth = rows * columns
    halves = columns // planes
    col = lax.axis_index("col")
    line = col // 2

    def across(x, bits):
        return lax.ppermute(x, "col", [(i, i ^ bits) for i in range(columns)])

    def along(x, moves):
        return lax.ppermute(x, "row", moves)

    eighth = width // 8

    def column_chunk(first, count):
        parts = []
        for h in range(halves):
            at = h * width + first * eighth
            parts.append(panel_factors[:, at : at + count * eighth])
        return jnp.stack(parts)

    after = lax.optimization_barrier

    everywhere = [lax.all_gather(column_chunk(*g), "row", axis=0, tiled=True) for g in GATHERS]
    cut = rows // 2
    own = [panel_factors[:cut], panel_factors[cut:]]
    gathered = [[own, None]] + [[[None, None], None] for _ in range(lines - 1)]
    single = [1 << i for i in range(lines.bit_length() - 1)]

    def early(s):
        return 0 if s == 1 else 1

    for s in single:
        gathered[s][0][early(s)] = across(own[early(s)], 2 * s)
    solved = lax.dot_general(
        vectors_t, inverse_lower_factors, (((2,), (2,)), ((0,), (0,))), precision=HIGHEST
    )
    cores = jnp.einsum("fdv,fpv->fdp", solved, solved, precision=HIGHEST)
    bit = 1
    while bit < planes:
        cores = cores + along(cores, [(i, i ^ bit) for i in range(planes)])
        bit *= 2

    mine = column_chunk(*HOPPED)
    from_above, from_below = [mine], [mine]

    def hop(d):
        from_above.append(along(from_above[-1], [(p, p - 1) for p in range(1, planes - d + 1)]))
        from_below.append(along(from_below[-1], [(p, p + 1) for p in range(d - 1, planes - 1)]))

    hop(1)

    arrived, cores, own, hopped = after(
        ([gathered[s][0][early(s)] for s in single], cores, own, (from_above[-1], from_below[-1]))
    )
    from_above[-1], from_below[-1] = hopped
    for s, x in zip(single, arrived):
        gathered[s][0][early(s)] = x
        gathered[s][0][1 - early(s)] = across(own[1 - early(s)], 2 * s)
    several = sorted((s for s in range(1, lines) if s not in single), key=lambda s: bin(s).count("1"))
    for s in several:
        low, high = s & -s, 1 << (s.bit_length() - 1)
        gathered[s][0] = [
            across(gathered[s ^ high][0][0], 2 * high),
            across(gathered[s ^ low][0][1], 2 * low),
        ]

    arrived, cores, everywhere[0], hopped = after(
        (
            [gathered[s][0] for s in range(1, lines)],
            cores,
            everywhere[0],
            (from_above[-1], from_below[-1]),
        )
    )
    from_above[-1], from_below[-1] = hopped
    for s, x in zip(range(1, lines), arrived):
        gathered[s][0] = x
    near = [cores] + [across(cores, 2 * s) for s in range(1, lines)]
    hop(2)
    far = across(jnp.concatenate(near), 1)
    blocks = diagonal_blocks(col.astype(jnp.int32).reshape(1), slot_of_panel, near, far)

    def scale(s, left):
        place = (line ^ s).astype(jnp.int32).reshape(1)
        groups = gathered[s][0], [across(x, 1) for x in gathered[s][0]]
        parts = [(x, 0) for group in groups for x in group]
        if s == 0:
            whole = [panel_factors, across(panel_factors, 1)]
            parts = [(x, half) for x in whole for half in range(2)]
        return scale_into(place, parts, blocks, s, left, depth)

    def exchange(number):
        chunk = lax.all_to_all(everywhere[number], "col", split_axis=0, concat_axis=0, tiled=True)
        return chunk.reshape(depth, -1)

    chunks = [exchange(0)]

    left, hopped = after((scale(0, None), (from_above[-1], from_below[-1])))
    from_above[-1], from_below[-1] = hopped
    for d in range(3, planes):
        hop(d)
    for s in range(1, lines):
        left = scale(s, left)
    plane = lax.axis_index("row").astype(jnp.int32).reshape(1)
    everywhere[1] = lay(plane, from_below[:0:-1] + [mine] + from_above[1:], everywhere[1])

    updated = None
    for number, (first, _) in enumerate(CHUNKS):
        later = number + 1
        if later < len(CHUNKS):
            if updated is None:
                everywhere[later], left = after((everywhere[later], left))
            else:
                everywhere[later], updated = after((everywhere[later], updated))
            chunks.append(exchange(later))
        updated = update_chunk(first * eighth, trailing, left, chunks[number], updated)
    return updated


def solution(mesh):
    planes, columns = mesh.shape["row"], mesh.shape["col"]
    if columns != 2 * planes or planes & (planes - 1):
        raise ValueError("unsupported mesh")
    return jax.shard_map(
        functools.partial(body, planes, columns),
        mesh=mesh,
        in_specs=(
            P("row", "col"),
            P("col", "row"),
            P("col", None, None),
            P("col", "row", None),
            P(),
        ),
        out_specs=P("row", "col"),
        check_vma=False,
    )
```

```python
import functools

import jax
import jax.numpy as jnp
from jax import lax
from jax.experimental import pallas as pl
from jax.experimental.pallas import tpu as pltpu
from jax.sharding import PartitionSpec as P

GATHERS = ((0, 3), (4, 2), (6, 2))
DIRECT = (3, 1)
CHUNKS = ((0, 3), (3, 3), (6, 2))
HIGHEST = lax.Precision.HIGHEST
SCALE_VMEM = 48 * 1024 * 1024
UPDATE_VMEM = 48 * 1024 * 1024
EARLY = pl.CostEstimate(flops=1, bytes_accessed=1, transcendentals=0)


def split(x):
    hi = x.astype(jnp.bfloat16)
    return hi, (x - hi.astype(jnp.float32)).astype(jnp.bfloat16)


def dot3(a_hi, a_lo, b_hi, b_lo):
    dot = functools.partial(jnp.dot, preferred_element_type=jnp.float32)
    return dot(a_hi, b_hi) + (dot(a_hi, b_lo) + dot(a_lo, b_hi))


def scale_kernel(place, *refs):
    parts, cores, (hi, lo) = refs[:4], refs[4], refs[-2:]
    group = jnp.concatenate([part[...] for part in parts], axis=0)
    scaled = dot3(*split(cores[0]), *split(group))
    hi[...], lo[...] = split(scaled.T)


def scale_into(place, parts, cores, line, previous, depth):
    width = parts[0][0].shape[1]
    rows = cores.shape[1]
    half = rows // 4
    tile = min(width, 1024)
    block = pl.BlockSpec((tile, rows), lambda i, place: (i, place[0]))
    shape = jax.ShapeDtypeStruct((width, depth), jnp.bfloat16)
    held = [] if previous is None else list(previous)
    return pl.pallas_call(
        scale_kernel,
        grid_spec=pltpu.PrefetchScalarGridSpec(
            num_scalar_prefetch=1,
            grid=(width // tile,),
            in_specs=[
                pl.BlockSpec((half, tile), functools.partial(lambda at, i, place: (at, i), at))
                for _, at in parts
            ]
            + [pl.BlockSpec((1, rows, rows), lambda i, place: (line, 0, 0))]
            + [pl.BlockSpec(memory_space=pl.ANY)] * len(held),
            out_specs=[block, block],
        ),
        out_shape=[shape, shape],
        input_output_aliases={} if previous is None else {6: 0, 7: 1},
        compiler_params=pltpu.CompilerParams(vmem_limit_bytes=SCALE_VMEM),
        cost_estimate=EARLY,
    )(place, *(a for a, _ in parts), cores, *held)


def blocks_kernel(per_col, col, slots, *refs):
    near, far, (out, held) = refs[:-3], refs[-3], refs[-2:]
    lines = len(near)
    rank = held.shape[1]
    together = 2 * per_col
    for s in range(lines):
        held[s * together : s * together + per_col] = near[s][...]
        held[s * together + per_col : (s + 1) * together] = far[s * per_col : (s + 1) * per_col]
    out[...] = jnp.zeros_like(out)
    me = col[0]
    for s in range(lines):
        for t in range(together):
            owner = me ^ (2 * s + t // per_col)
            slot = slots[owner * per_col + t % per_col]
            block = held[((slot // per_col) ^ me) * per_col + slot % per_col]
            row = (t + (me % 2) * per_col) % together
            out[s, pl.ds(pl.multiple_of(row * rank, rank), rank), t * rank : (t + 1) * rank] = block


def diagonal_blocks(col, slots, near, far):
    per_col, rank, _ = near[0].shape
    lines = len(near)
    size = 2 * per_col * rank
    return pl.pallas_call(
        functools.partial(blocks_kernel, per_col),
        grid_spec=pltpu.PrefetchScalarGridSpec(
            num_scalar_prefetch=2,
            grid=(1,),
            in_specs=[pl.BlockSpec(x.shape, lambda i, col, slots: (0, 0, 0)) for x in (*near, far)],
            out_specs=pl.BlockSpec((lines, size, size), lambda i, col, slots: (0, 0, 0)),
            scratch_shapes=[pltpu.VMEM((2 * lines * per_col, rank, rank), jnp.float32)],
        ),
        out_shape=jax.ShapeDtypeStruct((lines, size, size), jnp.float32),
        compiler_params=pltpu.CompilerParams(vmem_limit_bytes=SCALE_VMEM),
        cost_estimate=EARLY,
    )(col, slots, *near, far)


def lay_kernel(planes, plane, *refs):
    sources, rest, (out, sems) = refs[:planes], refs[-3], refs[-2:]
    blocks = out.shape[0] // planes
    wide = sources[0].shape[2]
    tail = pltpu.make_async_copy(rest, out.at[:, :, pl.ds(wide, rest.shape[2])], sems.at[planes])
    tail.start()
    for z in range(planes):

        @pl.when(plane[0] == z)
        def _():
            copies = [
                pltpu.make_async_copy(
                    sources[(z - q) % planes],
                    out.at[pl.ds(q * blocks, blocks), :, pl.ds(0, wide)],
                    sems.at[q],
                )
                for q in range(planes)
            ]
            for copy in copies:
                copy.start()
            for copy in copies:
                copy.wait()

    tail.wait()


def lay(plane, sources, rest):
    planes = len(sources)
    shape = sources[0].shape
    result = (rest.shape[0], shape[1], shape[2] + rest.shape[2])
    return pl.pallas_call(
        functools.partial(lay_kernel, planes),
        grid_spec=pltpu.PrefetchScalarGridSpec(
            num_scalar_prefetch=1,
            grid=(1,),
            in_specs=[pl.BlockSpec(memory_space=pl.ANY)] * (len(sources) + 1),
            out_specs=pl.BlockSpec(result, lambda i, plane: (0, 0, 0)),
            scratch_shapes=[pltpu.SemaphoreType.DMA((planes + 1,))],
        ),
        out_shape=jax.ShapeDtypeStruct(result, jnp.float32),
        compiler_params=pltpu.CompilerParams(vmem_limit_bytes=SCALE_VMEM),
        cost_estimate=EARLY,
    )(plane, *sources, rest)


def update_kernel(trailing, hi, lo, right, *refs):
    out, right_hi, right_lo = refs[-3:]

    @pl.when(pl.program_id(0) == 0)
    def _():
        right_hi[...], right_lo[...] = split(right[...])

    out[...] = trailing[...] - dot3(hi[...], lo[...], right_hi[...], right_lo[...])


def update_chunk(start, trailing, left, right, previous):
    height = trailing.shape[0]
    depth, wide = right.shape
    tile = min(height, 1024)
    here = pl.BlockSpec((tile, wide), lambda i: (i, start // wide))
    side = pl.BlockSpec((tile, depth), lambda i: (i, 0))
    held = [] if previous is None else [previous]
    return pl.pallas_call(
        update_kernel,
        grid=(height // tile,),
        in_specs=[here, side, side, pl.BlockSpec((depth, wide), lambda i: (0, 0))]
        + [pl.BlockSpec(memory_space=pl.ANY)] * len(held),
        out_specs=here,
        out_shape=jax.ShapeDtypeStruct(trailing.shape, jnp.float32),
        scratch_shapes=[pltpu.VMEM((depth, wide), jnp.bfloat16)] * 2,
        input_output_aliases={} if previous is None else {4: 0},
        compiler_params=pltpu.CompilerParams(vmem_limit_bytes=UPDATE_VMEM),
        cost_estimate=EARLY,
    )(trailing, *left, right, *held)


def body(planes, columns, trailing, panel_factors, vectors_t, inverse_lower_factors, slot_of_panel):
    lines = columns // 2
    rows = panel_factors.shape[0]
    width = trailing.shape[1]
    depth = rows * columns
    halves = columns // planes
    col = lax.axis_index("col")
    line = col // 2

    def across(x, bits):
        return lax.ppermute(x, "col", [(i, i ^ bits) for i in range(columns)])

    def along(x, moves):
        return lax.ppermute(x, "row", moves)

    eighth = width // 8

    def column_chunk(first, count):
        parts = []
        for h in range(halves):
            at = h * width + first * eighth
            parts.append(panel_factors[:, at : at + count * eighth])
        return jnp.stack(parts)

    after = lax.optimization_barrier

    everywhere = [lax.all_gather(column_chunk(*g), "row", axis=0, tiled=True) for g in GATHERS]
    cut = rows // 2
    own = [panel_factors[:cut], panel_factors[cut:]]
    gathered = [[own, None]] + [[[None, None], None] for _ in range(lines - 1)]
    single = [1 << i for i in range(lines.bit_length() - 1)]

    def early(s):
        return 0 if s == 1 else 1

    for s in single:
        gathered[s][0][early(s)] = across(own[early(s)], 2 * s)
    solved = lax.dot_general(
        vectors_t, inverse_lower_factors, (((2,), (2,)), ((0,), (0,))), precision=HIGHEST
    )
    cores = jnp.einsum("fdv,fpv->fdp", solved, solved, precision=HIGHEST)
    bit = 1
    while bit < planes:
        cores = cores + along(cores, [(i, i ^ bit) for i in range(planes)])
        bit *= 2

    arrived, cores, own = after(([gathered[s][0][early(s)] for s in single], cores, own))
    near = [cores] + [across(cores, 2 * s) for s in range(1, lines)]
    for s, x in zip(single, arrived):
        gathered[s][0][early(s)] = x
        gathered[s][0][1 - early(s)] = across(own[1 - early(s)], 2 * s)
    several = sorted((s for s in range(1, lines) if s not in single), key=lambda s: bin(s).count("1"))
    for s in several:
        low, high = s & -s, 1 << (s.bit_length() - 1)
        gathered[s][0] = [
            across(gathered[s ^ high][0][0], 2 * high),
            across(gathered[s ^ low][0][1], 2 * low),
        ]

    mine = column_chunk(*DIRECT)
    arrived, near, everywhere[0], mine = after(
        ([gathered[s][0] for s in range(1, lines)], near, everywhere[0], mine)
    )
    for s, x in zip(range(1, lines), arrived):
        gathered[s][0] = x
    direct = [mine] + [
        along(mine, [(p, (p + d) % planes) for p in range(planes)]) for d in range(1, planes)
    ]
    far = across(jnp.concatenate(near), 1)
    blocks = diagonal_blocks(col.astype(jnp.int32).reshape(1), slot_of_panel, near, far)

    def scale(s, left):
        place = (line ^ s).astype(jnp.int32).reshape(1)
        groups = gathered[s][0], [across(x, 1) for x in gathered[s][0]]
        parts = [(x, 0) for group in groups for x in group]
        if s == 0:
            whole = [panel_factors, across(panel_factors, 1)]
            parts = [(x, half) for x in whole for half in range(2)]
        return scale_into(place, parts, blocks, s, left, depth)

    def exchange(number):
        chunk = lax.all_to_all(everywhere[number], "col", split_axis=0, concat_axis=0, tiled=True)
        return chunk.reshape(depth, -1)

    chunks = [exchange(0)]

    left = None
    for s in range(lines - 1):
        left = scale(s, left)
    left, direct = after((left, direct))
    left = scale(lines - 1, left)
    plane = lax.axis_index("row").astype(jnp.int32).reshape(1)
    everywhere[1] = lay(plane, direct, everywhere[1])

    updated = None
    for number, (first, _) in enumerate(CHUNKS):
        later = number + 1
        if later < len(CHUNKS):
            if updated is None:
                everywhere[later], left = after((everywhere[later], left))
            else:
                everywhere[later], updated = after((everywhere[later], updated))
            chunks.append(exchange(later))
        updated = update_chunk(first * eighth, trailing, left, chunks[number], updated)
    return updated


def solution(mesh):
    planes, columns = mesh.shape["row"], mesh.shape["col"]
    if columns != 2 * planes or planes & (planes - 1):
        raise ValueError("unsupported mesh")
    return jax.shard_map(
        functools.partial(body, planes, columns),
        mesh=mesh,
        in_specs=(
            P("row", "col"),
            P("col", "row"),
            P("col", None, None),
            P("col", "row", None),
            P(),
        ),
        out_specs=P("row", "col"),
        check_vma=False,
    )
```

```python
import functools

import jax
import jax.numpy as jnp
from jax import lax
from jax.experimental import pallas as pl
from jax.experimental.pallas import tpu as pltpu
from jax.sharding import PartitionSpec as P

CHUNKS = ((0, 3), (3, 3), (6, 2))
HIGHEST = lax.Precision.HIGHEST
SCALE_VMEM = 48 * 1024 * 1024
UPDATE_VMEM = 48 * 1024 * 1024
EARLY = pl.CostEstimate(flops=1, bytes_accessed=1, transcendentals=0)


def split(x):
    hi = x.astype(jnp.bfloat16)
    return hi, (x - hi.astype(jnp.float32)).astype(jnp.bfloat16)


def dot3(a_hi, a_lo, b_hi, b_lo):
    dot = functools.partial(jnp.dot, preferred_element_type=jnp.float32)
    return dot(a_hi, b_hi) + (dot(a_hi, b_lo) + dot(a_lo, b_hi))


def scale_kernel(place, *refs):
    parts, cores, (out, low) = refs[:4], refs[4], refs[-2:]

    @pl.when(pl.program_id(1) == 0)
    def _():
        group = jnp.concatenate([part[...] for part in parts], axis=0)
        scaled = dot3(*split(cores[0]), *split(group))
        out[...], low[...] = split(scaled.T)

    @pl.when(pl.program_id(1) == 1)
    def _():
        out[...] = low[...]


def scale_into(place, parts, cores, line, previous, depth):
    width = parts[0][0].shape[1]
    rows = cores.shape[1]
    half = rows // 4
    tile = min(width, 1024)
    held = [] if previous is None else [previous]
    return pl.pallas_call(
        scale_kernel,
        grid_spec=pltpu.PrefetchScalarGridSpec(
            num_scalar_prefetch=1,
            grid=(width // tile, 2),
            in_specs=[
                pl.BlockSpec((half, tile), functools.partial(lambda at, i, j, place: (at, i), at))
                for _, at in parts
            ]
            + [pl.BlockSpec((1, rows, rows), lambda i, j, place: (line, 0, 0))]
            + [pl.BlockSpec(memory_space=pl.ANY)] * len(held),
            out_specs=pl.BlockSpec((tile, rows), lambda i, j, place: (i, place[0] + j * (depth // rows))),
            scratch_shapes=[pltpu.VMEM((tile, rows), jnp.bfloat16)],
        ),
        out_shape=jax.ShapeDtypeStruct((width, 2 * depth), jnp.bfloat16),
        input_output_aliases={} if previous is None else {6: 0},
        compiler_params=pltpu.CompilerParams(vmem_limit_bytes=SCALE_VMEM),
        cost_estimate=EARLY,
    )(place, *(a for a, _ in parts), cores, *held)


def blocks_kernel(per_col, col, slots, *refs):
    near, far, (out, held) = refs[:-3], refs[-3], refs[-2:]
    lines = len(near)
    rank = held.shape[1]
    together = 2 * per_col
    for s in range(lines):
        held[s * together : s * together + per_col] = near[s][...]
        held[s * together + per_col : (s + 1) * together] = far[s * per_col : (s + 1) * per_col]
    out[...] = jnp.zeros_like(out)
    me = col[0]
    for s in range(lines):
        for t in range(together):
            owner = me ^ (2 * s + t // per_col)
            slot = slots[owner * per_col + t % per_col]
            block = held[((slot // per_col) ^ me) * per_col + slot % per_col]
            row = (t + (me % 2) * per_col) % together
            out[s, pl.ds(pl.multiple_of(row * rank, rank), rank), t * rank : (t + 1) * rank] = block


def diagonal_blocks(col, slots, near, far):
    per_col, rank, _ = near[0].shape
    lines = len(near)
    size = 2 * per_col * rank
    return pl.pallas_call(
        functools.partial(blocks_kernel, per_col),
        grid_spec=pltpu.PrefetchScalarGridSpec(
            num_scalar_prefetch=2,
            grid=(1,),
            in_specs=[pl.BlockSpec(x.shape, lambda i, col, slots: (0, 0, 0)) for x in (*near, far)],
            out_specs=pl.BlockSpec((lines, size, size), lambda i, col, slots: (0, 0, 0)),
            scratch_shapes=[pltpu.VMEM((2 * lines * per_col, rank, rank), jnp.float32)],
        ),
        out_shape=jax.ShapeDtypeStruct((lines, size, size), jnp.float32),
        compiler_params=pltpu.CompilerParams(vmem_limit_bytes=SCALE_VMEM),
        cost_estimate=EARLY,
    )(col, slots, *near, far)


def update_kernel(trailing, left, right, *refs):
    out, twice, low = refs[-3:]
    depth = right.shape[0]

    @pl.when(pl.program_id(0) == 0)
    def _():
        high, low[...] = split(right[...])
        twice[:depth] = high
        twice[depth:] = high

    dot = functools.partial(jnp.dot, preferred_element_type=jnp.float32)
    out[...] = trailing[...] - (dot(left[...], twice[...]) + dot(left[:, :depth], low[...]))


def update_chunk(start, trailing, left, right, previous):
    height = trailing.shape[0]
    depth, wide = right.shape
    tile = min(height, 1024)
    here = pl.BlockSpec((tile, wide), lambda i: (i, start // wide))
    held = [] if previous is None else [previous]
    return pl.pallas_call(
        update_kernel,
        grid=(height // tile,),
        in_specs=[
            here,
            pl.BlockSpec((tile, 2 * depth), lambda i: (i, 0)),
            pl.BlockSpec((depth, wide), lambda i: (0, 0)),
        ]
        + [pl.BlockSpec(memory_space=pl.ANY)] * len(held),
        out_specs=here,
        out_shape=jax.ShapeDtypeStruct(trailing.shape, jnp.float32),
        scratch_shapes=[
            pltpu.VMEM((2 * depth, wide), jnp.bfloat16),
            pltpu.VMEM((depth, wide), jnp.bfloat16),
        ],
        input_output_aliases={} if previous is None else {3: 0},
        compiler_params=pltpu.CompilerParams(vmem_limit_bytes=UPDATE_VMEM),
        cost_estimate=EARLY,
    )(trailing, left, right, *held)


def body(planes, columns, trailing, panel_factors, vectors_t, inverse_lower_factors, slot_of_panel):
    lines = columns // 2
    rows = panel_factors.shape[0]
    width = trailing.shape[1]
    depth = rows * columns
    halves = columns // planes
    col = lax.axis_index("col")
    line = col // 2

    def across(x, bits):
        return lax.ppermute(x, "col", [(i, i ^ bits) for i in range(columns)])

    def along(x, moves):
        return lax.ppermute(x, "row", moves)

    eighth = width // 8

    def column_chunk(first, count):
        parts = []
        for h in range(halves):
            at = h * width + first * eighth
            parts.append(panel_factors[:, at : at + count * eighth])
        return jnp.stack(parts)

    after = lax.optimization_barrier

    everywhere = [lax.all_gather(column_chunk(*g), "row", axis=0, tiled=True) for g in CHUNKS]
    cut = rows // 2
    own = [panel_factors[:cut], panel_factors[cut:]]
    gathered = [[own, None]] + [[[None, None], None] for _ in range(lines - 1)]
    single = [1 << i for i in range(lines.bit_length() - 1)]

    def early(s):
        return 0 if s == 1 else 1

    for s in single:
        gathered[s][0][early(s)] = across(own[early(s)], 2 * s)
    solved = lax.dot_general(
        vectors_t, inverse_lower_factors, (((2,), (2,)), ((0,), (0,))), precision=HIGHEST
    )
    cores = jnp.einsum("fdv,fpv->fdp", solved, solved, precision=HIGHEST)
    bit = 1
    while bit < planes:
        cores = cores + along(cores, [(i, i ^ bit) for i in range(planes)])
        bit *= 2

    near = [cores] + [across(cores, 2 * s) for s in range(1, lines)]

    arrived, near, own = after(([gathered[s][0][early(s)] for s in single], near, own))
    for s, x in zip(single, arrived):
        gathered[s][0][early(s)] = x
        gathered[s][0][1 - early(s)] = across(own[1 - early(s)], 2 * s)
    several = sorted((s for s in range(1, lines) if s not in single), key=lambda s: bin(s).count("1"))
    for s in several:
        low, high = s & -s, 1 << (s.bit_length() - 1)
        gathered[s][0] = [
            across(gathered[s ^ high][0][0], 2 * high),
            across(gathered[s ^ low][0][1], 2 * low),
        ]

    arrived, near, everywhere[0] = after(
        ([gathered[s][0] for s in range(1, lines)], near, everywhere[0])
    )
    for s, x in zip(range(1, lines), arrived):
        gathered[s][0] = x
    far = across(jnp.concatenate(near), 1)
    blocks = diagonal_blocks(col.astype(jnp.int32).reshape(1), slot_of_panel, near, far)

    def scale(s, left):
        place = (line ^ s).astype(jnp.int32).reshape(1)
        groups = gathered[s][0], [across(x, 1) for x in gathered[s][0]]
        parts = [(x, 0) for group in groups for x in group]
        if s == 0:
            whole = [panel_factors, across(panel_factors, 1)]
            parts = [(x, half) for x in whole for half in range(2)]
        return scale_into(place, parts, blocks, s, left, depth)

    def exchange(number):
        chunk = lax.all_to_all(everywhere[number], "col", split_axis=0, concat_axis=0, tiled=True)
        return chunk.reshape(depth, -1)

    chunks = [exchange(0)]

    left = None
    for s in range(lines):
        left = scale(s, left)

    updated = None
    for number, (first, _) in enumerate(CHUNKS):
        later = number + 1
        if later < len(CHUNKS):
            if updated is None:
                everywhere[later], left = after((everywhere[later], left))
            else:
                everywhere[later], updated = after((everywhere[later], updated))
            chunks.append(exchange(later))
        updated = update_chunk(first * eighth, trailing, left, chunks[number], updated)
    return updated


def solution(mesh):
    planes, columns = mesh.shape["row"], mesh.shape["col"]
    if columns != 2 * planes or planes & (planes - 1):
        raise ValueError("unsupported mesh")
    return jax.shard_map(
        functools.partial(body, planes, columns),
        mesh=mesh,
        in_specs=(
            P("row", "col"),
            P("col", "row"),
            P("col", None, None),
            P("col", "row", None),
            P(),
        ),
        out_specs=P("row", "col"),
        check_vma=False,
    )
```

```python
import functools

import jax
import jax.numpy as jnp
from jax import lax
from jax.experimental import pallas as pl
from jax.experimental.pallas import tpu as pltpu
from jax.sharding import PartitionSpec as P

CHUNKS = ((0, 2), (3, 3), (6, 2), (2, 1))
HIGHEST = lax.Precision.HIGHEST
SCALE_VMEM = 48 * 1024 * 1024
UPDATE_VMEM = 48 * 1024 * 1024
EARLY = pl.CostEstimate(flops=1, bytes_accessed=1, transcendentals=0)


def split(x):
    hi = x.astype(jnp.bfloat16)
    return hi, (x - hi.astype(jnp.float32)).astype(jnp.bfloat16)


def dot3(a_hi, a_lo, b_hi, b_lo):
    dot = functools.partial(jnp.dot, preferred_element_type=jnp.float32)
    return dot(a_hi, b_hi) + (dot(a_hi, b_lo) + dot(a_lo, b_hi))


def scale_kernel(place, *refs):
    parts, cores, (hi, lo) = refs[:4], refs[4], refs[-2:]
    group = jnp.concatenate([part[...] for part in parts], axis=0)
    scaled = dot3(*split(cores[0]), *split(group))
    hi[...], lo[...] = split(scaled.T)


def scale_into(place, parts, cores, line, previous, depth):
    width = parts[0][0].shape[1]
    rows = cores.shape[1]
    half = rows // 4
    tile = min(width, 1024)
    block = pl.BlockSpec((tile, rows), lambda i, place: (i, place[0]))
    shape = jax.ShapeDtypeStruct((width, depth), jnp.bfloat16)
    held = [] if previous is None else list(previous)
    return pl.pallas_call(
        scale_kernel,
        grid_spec=pltpu.PrefetchScalarGridSpec(
            num_scalar_prefetch=1,
            grid=(width // tile,),
            in_specs=[
                pl.BlockSpec((half, tile), functools.partial(lambda at, i, place: (at, i), at))
                for _, at in parts
            ]
            + [pl.BlockSpec((1, rows, rows), lambda i, place: (line, 0, 0))]
            + [pl.BlockSpec(memory_space=pl.ANY)] * len(held),
            out_specs=[block, block],
        ),
        out_shape=[shape, shape],
        input_output_aliases={} if previous is None else {6: 0, 7: 1},
        compiler_params=pltpu.CompilerParams(vmem_limit_bytes=SCALE_VMEM),
        cost_estimate=EARLY,
    )(place, *(a for a, _ in parts), cores, *held)


def blocks_kernel(per_col, col, slots, *refs):
    near, far, (out, held) = refs[:-3], refs[-3], refs[-2:]
    lines = len(near)
    rank = held.shape[1]
    together = 2 * per_col
    for s in range(lines):
        held[s * together : s * together + per_col] = near[s][...]
        held[s * together + per_col : (s + 1) * together] = far[s * per_col : (s + 1) * per_col]
    out[...] = jnp.zeros_like(out)
    me = col[0]
    for s in range(lines):
        for t in range(together):
            owner = me ^ (2 * s + t // per_col)
            slot = slots[owner * per_col + t % per_col]
            block = held[((slot // per_col) ^ me) * per_col + slot % per_col]
            row = (t + (me % 2) * per_col) % together
            out[s, pl.ds(pl.multiple_of(row * rank, rank), rank), t * rank : (t + 1) * rank] = block


def diagonal_blocks(col, slots, near, far):
    per_col, rank, _ = near[0].shape
    lines = len(near)
    size = 2 * per_col * rank
    return pl.pallas_call(
        functools.partial(blocks_kernel, per_col),
        grid_spec=pltpu.PrefetchScalarGridSpec(
            num_scalar_prefetch=2,
            grid=(1,),
            in_specs=[pl.BlockSpec(x.shape, lambda i, col, slots: (0, 0, 0)) for x in (*near, far)],
            out_specs=pl.BlockSpec((lines, size, size), lambda i, col, slots: (0, 0, 0)),
            scratch_shapes=[pltpu.VMEM((2 * lines * per_col, rank, rank), jnp.float32)],
        ),
        out_shape=jax.ShapeDtypeStruct((lines, size, size), jnp.float32),
        compiler_params=pltpu.CompilerParams(vmem_limit_bytes=SCALE_VMEM),
        cost_estimate=EARLY,
    )(col, slots, *near, far)


def update_kernel(trailing, hi, lo, right, *refs):
    out, right_hi, right_lo = refs[-3:]

    @pl.when(pl.program_id(0) == 0)
    def _():
        right_hi[...], right_lo[...] = split(right[...])

    out[...] = trailing[...] - dot3(hi[...], lo[...], right_hi[...], right_lo[...])


def update_chunk(start, trailing, left, right, previous):
    height = trailing.shape[0]
    depth, wide = right.shape
    tile = min(height, 1024)
    here = pl.BlockSpec((tile, wide), lambda i: (i, start // wide))
    side = pl.BlockSpec((tile, depth), lambda i: (i, 0))
    held = [] if previous is None else [previous]
    return pl.pallas_call(
        update_kernel,
        grid=(height // tile,),
        in_specs=[here, side, side, pl.BlockSpec((depth, wide), lambda i: (0, 0))]
        + [pl.BlockSpec(memory_space=pl.ANY)] * len(held),
        out_specs=here,
        out_shape=jax.ShapeDtypeStruct(trailing.shape, jnp.float32),
        scratch_shapes=[pltpu.VMEM((depth, wide), jnp.bfloat16)] * 2,
        input_output_aliases={} if previous is None else {4: 0},
        compiler_params=pltpu.CompilerParams(vmem_limit_bytes=UPDATE_VMEM),
        cost_estimate=EARLY,
    )(trailing, *left, right, *held)


def body(planes, columns, trailing, panel_factors, vectors_t, inverse_lower_factors, slot_of_panel):
    lines = columns // 2
    rows = panel_factors.shape[0]
    width = trailing.shape[1]
    depth = rows * columns
    halves = columns // planes
    col = lax.axis_index("col")
    line = col // 2

    def across(x, bits):
        return lax.ppermute(x, "col", [(i, i ^ bits) for i in range(columns)])

    def along(x, moves):
        return lax.ppermute(x, "row", moves)

    eighth = width // 8

    def column_chunk(first, count):
        parts = []
        for h in range(halves):
            at = h * width + first * eighth
            parts.append(panel_factors[:, at : at + count * eighth])
        return jnp.stack(parts)

    after = lax.optimization_barrier

    everywhere = [lax.all_gather(column_chunk(*g), "row", axis=0, tiled=True) for g in CHUNKS]
    cut = rows // 2
    own = [panel_factors[:cut], panel_factors[cut:]]
    gathered = [[own, None]] + [[[None, None], None] for _ in range(lines - 1)]
    single = [1 << i for i in range(lines.bit_length() - 1)]

    def early(s):
        return 0 if s == 1 else 1

    for s in single:
        gathered[s][0][early(s)] = across(own[early(s)], 2 * s)
    solved = lax.dot_general(
        vectors_t, inverse_lower_factors, (((2,), (2,)), ((0,), (0,))), precision=HIGHEST
    )
    cores = jnp.einsum("fdv,fpv->fdp", solved, solved, precision=HIGHEST)
    bit = 1
    while bit < planes:
        cores = cores + along(cores, [(i, i ^ bit) for i in range(planes)])
        bit *= 2

    near = [cores] + [across(cores, 2 * s) for s in range(1, lines)]

    arrived, near, own = after(([gathered[s][0][early(s)] for s in single], near, own))
    for s, x in zip(single, arrived):
        gathered[s][0][early(s)] = x
        gathered[s][0][1 - early(s)] = across(own[1 - early(s)], 2 * s)
    several = sorted((s for s in range(1, lines) if s not in single), key=lambda s: bin(s).count("1"))
    for s in several:
        low, high = s & -s, 1 << (s.bit_length() - 1)
        gathered[s][0] = [
            across(gathered[s ^ high][0][0], 2 * high),
            across(gathered[s ^ low][0][1], 2 * low),
        ]

    arrived, near, everywhere[0] = after(
        ([gathered[s][0] for s in range(1, lines)], near, everywhere[0])
    )
    for s, x in zip(range(1, lines), arrived):
        gathered[s][0] = x
    far = across(jnp.concatenate(near), 1)
    blocks = diagonal_blocks(col.astype(jnp.int32).reshape(1), slot_of_panel, near, far)

    def scale(s, left):
        place = (line ^ s).astype(jnp.int32).reshape(1)
        groups = gathered[s][0], [across(x, 1) for x in gathered[s][0]]
        parts = [(x, 0) for group in groups for x in group]
        if s == 0:
            whole = [panel_factors, across(panel_factors, 1)]
            parts = [(x, half) for x in whole for half in range(2)]
        return scale_into(place, parts, blocks, s, left, depth)

    def exchange(number):
        chunk = lax.all_to_all(everywhere[number], "col", split_axis=0, concat_axis=0, tiled=True)
        return chunk.reshape(depth, -1)

    chunks = [exchange(0)]

    left = None
    for s in range(lines - 1):
        left = scale(s, left)
    everywhere[1], left = after((everywhere[1], left))
    chunks.append(exchange(1))
    left = scale(lines - 1, left)

    updated = None
    for number, (first, _) in enumerate(CHUNKS):
        later = number + 1
        if 1 < later < len(CHUNKS):
            everywhere[later], updated = after((everywhere[later], updated))
            chunks.append(exchange(later))
        updated = update_chunk(first * eighth, trailing, left, chunks[number], updated)
    return updated


def solution(mesh):
    planes, columns = mesh.shape["row"], mesh.shape["col"]
    if columns != 2 * planes or planes & (planes - 1):
        raise ValueError("unsupported mesh")
    return jax.shard_map(
        functools.partial(body, planes, columns),
        mesh=mesh,
        in_specs=(
            P("row", "col"),
            P("col", "row"),
            P("col", None, None),
            P("col", "row", None),
            P(),
        ),
        out_specs=P("row", "col"),
        check_vma=False,
    )
```
